32 devices in a mesh: groups: 2 (over x), dom: 16 (over z, y, core).
Axes of the slice: x: 2, y: 2, z: 4, core: 2. Of those that a mesh axis runs over, the one named last changes fastest.
Arguments:
- fine_latent: bfloat16 [131072, 128], P(('groups', 'dom')), parts along dimension 0, may hold values from -6 to 6
- fine_edges: bfloat16 [524288, 128], P(('groups', 'dom')), parts along dimension 0, may hold values from -6 to 6
- fine_sender: int32 [524288], P(('groups', 'dom')), parts along dimension 0, may hold values from 0 to 6143
- fine_receiver: int32 [524288], P(('groups', 'dom')), parts along dimension 0, may hold values from 0 to 4095, as said below
- edge_count: int32 [32], P(('groups', 'dom')), parts along dimension 0, may hold values from 8192 to 16384, as said below
- fine_border: int32 [32, 2, 1024], P(('groups', 'dom')), parts along dimension 0, may hold values from 0 to 4095
- pool_rows: int32 [32, 2, 512], P(('groups', 'dom')), parts along dimension 0, may hold values from 0 to 4095
- pool_target: int32 [32, 2, 512], P(('groups', 'dom')), parts along dimension 0, may hold values from 0 to 511
- pool_weight: int32 [32, 2, 512], P(('groups', 'dom')), parts along dimension 0, may hold values from 0 to 4, as said below
- fine_parent: int32 [131072], P(('groups', 'dom')), parts along dimension 0, may hold values from 0 to 511, as said below
- fine_weight: int32 [131072], P(('groups', 'dom')), parts along dimension 0, may hold values from 1 to 4
- coarse_edges: bfloat16 [65536, 128], P(('groups', 'dom')), parts along dimension 0, may hold values from -6 to 6
- coarse_sender: int32 [65536], P(('groups', 'dom')), parts along dimension 0, may hold values from 0 to 767
- coarse_receiver: int32 [65536], P(('groups', 'dom')), parts along dimension 0, may hold values from 0 to 511, as said below
- coarse_border: int32 [32, 2, 128], P(('groups', 'dom')), parts along dimension 0, may hold values from 0 to 511
- coarse_parent: int32 [16384], P(('groups', 'dom')), parts along dimension 0, may hold values from 0 to 1023, as said below
- coarse_weight: int32 [16384], P(('groups', 'dom')), parts along dimension 0, may hold values from 1 to 4
- top_edges: bfloat16 [4096, 128], P('groups'), parts along dimension 0, may hold values from -6 to 6
- top_sender: int32 [4096], P('groups'), parts along dimension 0, may hold values from 0 to 1023
- top_receiver: int32 [4096], P('groups'), parts along dimension 0, may hold values from 0 to 1023, as said below
- edge_in: bfloat16 [3, 384, 128], replicated, may hold values from -0.3125 to 0.3125
- edge_out: bfloat16 [3, 128, 128], replicated, may hold values from -0.5 to 0.5
- node_in: bfloat16 [3, 256, 128], replicated, may hold values from -0.375 to 0.375
- node_out: bfloat16 [3, 128, 128], replicated, may hold values from -0.5 to 0.5
- norm_gain: float32 [3, 2, 128], replicated, may hold values from 0.1 to 1.9
Outputs:
- fine_out: bfloat16 [131072, 128], P(('groups', 'dom')), parts along dimension 0
- coarse_out: bfloat16 [16384, 128], P(('groups', 'dom')), parts along dimension 0
The draws below stay inside these ranges and needn't reach their ends.
There are 2 independent parts, one for each index of `groups`. The reference program is written for one: setup_inputs(seed, part) draws one part's arguments, and reference() takes and returns one part's arrays. A program takes and returns all parts, laid end to end along the dimension named above; an argument that names none is the same for every part. Nothing has to cross between parts.
Inputs may be any that keep to these rules, and one draw needn't show every extreme that they name: `edge_count`: one partition of each mesh has all 16384 edge slots live. `pool_weight`: weight 0 marks an empty slot; for each owner and side the live slots come first; slots from a partition that does not exist are empty. One owner of each mesh receives all 512 slots live from both neighbours. `fine_parent`: every level-1 row of a partition is the parent of at least four of its fine rows. `coarse_parent`: A level-1 node of partition d has its parent among level-2 nodes (d - 1) * 64 to (d + 2) * 64 - 1; every level-2 node j is the parent of at least four level-1 nodes of partition j // 64. `fine_receiver`: A partition's fine edge slots come in aligned tiles of b = min(128, 16384) slots; the receivers of tile t lie among local rows t w to (t + 1) w - 1, with w = b * 4096 // 16384. `coarse_receiver`: A partition's level-1 edges come in aligned tiles of b = min(128, 2048) edges; the receivers of tile t lie among local rows t w to (t + 1) w - 1, with w = b * 512 // 2048. `top_receiver`: Level-2 edges come in aligned tiles of b = min(128, 2048) edges; the receivers of tile t lie among rows t w to (t + 1) w - 1, with w = b * 1024 // 2048.
All inputs are finite; a program needn't handle non-finite values.
Results may differ from the reference program's by a relative error of at most 0.011.
Values may be sent and summed in bfloat16 or wider, within the bound.
No kernel may reach another device: no remote copies, remote signals or barrier semaphores. Data moves between devices by JAX's collectives and lax.ppermute only.
A program may use at most 128 MiB of HBM per device.

```python
import jax
import jax.numpy as jnp
from jax import lax

L = 128
NF_DEV = 4096
LEVELS = 3
N1_DEV = 512
HS = 1024
HS1 = 128
NE_DEV = 16384
NE1_DEV = 2048
CAP = 512
N2 = 1024
NE2 = 2048
NF = 65536
N1 = 8192
NE = 262144
NE1 = 32768
N_DOM = 16


def draw_edge_count(key, part):
    key = jax.random.fold_in(key, 11)
    first, second = jax.random.split(key)
    counts = jax.random.randint(first, (N_DOM,), NE_DEV // 2, NE_DEV + 1)
    busiest = jax.random.randint(second, (), 0, N_DOM)
    return jnp.where(jnp.arange(N_DOM) == busiest, NE_DEV, counts).astype(jnp.int32)


def draw_pool_weight(key, part):
    key = jax.random.fold_in(key, 17)
    keys = jax.random.split(key, 3)
    live_count = jax.random.randint(keys[0], (N_DOM, 2), CAP // 3, CAP + 1)
    busiest = jax.random.randint(keys[1], (), 1, N_DOM - 1)
    owner_index = jnp.arange(N_DOM)[:, None]
    side_index = jnp.arange(2)[None, :]
    live_count = jnp.where(owner_index == busiest, CAP, live_count)
    missing = (owner_index == 0) & (side_index == 0) | (owner_index == N_DOM - 1) & (side_index == 1)
    live_count = jnp.where(missing, 0, live_count)
    weights = jax.random.randint(keys[2], (N_DOM, 2, CAP), 1, 5)
    slot_index = jnp.arange(CAP)[None, None, :]
    return jnp.where(slot_index < live_count[:, :, None], weights, 0).astype(jnp.int32)


def block_parents(key, rows, own_base, spare_low, spare_high):
    first, second = jax.random.split(key)
    orders = jax.vmap(lambda sub_key: jax.random.permutation(sub_key, rows))(jax.random.split(first, N_DOM))
    spare = jax.random.randint(second, (N_DOM, rows), spare_low[:, None], spare_high[:, None])
    parents = jnp.where(orders < rows // 2, own_base[:, None] + orders // 4, spare)
    return parents.reshape(N_DOM * rows).astype(jnp.int32)


def draw_fine_parent(key, part):
    key = jax.random.fold_in(key, 23)
    zeros = jnp.zeros((N_DOM,), jnp.int32)
    return block_parents(key, NF_DEV, zeros, zeros, zeros + N1_DEV)


def draw_coarse_parent(key, part):
    key = jax.random.fold_in(key, 29)
    block = N1_DEV // 8
    owners = jnp.arange(N_DOM, dtype=jnp.int32)
    low = jnp.maximum(owners - 1, 0) * block
    high = jnp.minimum(owners + 2, N_DOM) * block
    return block_parents(key, N1_DEV, owners * block, low, high)


def tiled_receivers(key, copies, edges_each, rows_each):
    tile_rows = min(128, edges_each)
    window = tile_rows * rows_each // edges_each
    slots = jnp.arange(copies * edges_each, dtype=jnp.int32) % edges_each
    offsets = slots // tile_rows * window
    return (offsets + jax.random.randint(key, (copies * edges_each,), 0, window)).astype(jnp.int32)


def draw_fine_receiver(key, part):
    key = jax.random.fold_in(key, 31)
    return tiled_receivers(key, N_DOM, NE_DEV, NF_DEV)


def draw_coarse_receiver(key, part):
    key = jax.random.fold_in(key, 37)
    return tiled_receivers(key, N_DOM, NE1_DEV, N1_DEV)


def draw_top_receiver(key, part):
    key = jax.random.fold_in(key, 41)
    return tiled_receivers(key, 1, NE2, N2)


def with_ends(drawn, key, smallest, top_value):
    dims = drawn.shape
    place = [jax.random.randint(jax.random.fold_in(key, axis), (), 0, dims[axis]) for axis in range(len(dims))]
    drawn = drawn.at[tuple(place)].set(smallest)
    longest = dims.index(max(dims))
    place[longest] = (place[longest] + 1) % dims[longest]
    return drawn.at[tuple(place)].set(top_value)


def block_levels(stream_key, extent, cuts, least, top_value):
    def one(axis_at, blocks):
        heights = jax.random.uniform(jax.random.fold_in(jax.random.fold_in(stream_key, 6), axis_at), (blocks,), jnp.float32, least / len(cuts), top_value / len(cuts))
        return jnp.repeat(jnp.exp(heights), extent[axis_at] // blocks).reshape((-1,) + (1,) * (len(extent) - axis_at - 1))

    factor_of = one(*cuts[0])
    for cut in cuts[1:]:
        factor_of = factor_of * one(*cut)
    return factor_of


def bell_draw(own_key, extent, scale, reach, cuts=(), held_as=jnp.bfloat16):
    gain = block_levels(own_key, extent, cuts, -0.22, 0.18) if cuts else 1.0
    drawn = jax.random.normal(own_key, extent, jnp.float32) * scale * gain
    return jnp.minimum(jnp.maximum(drawn, -reach), reach).astype(held_as)


def setup_inputs(seed: int = 0, part: int = 0) -> dict:
    key_of = jax.random.split(jax.random.key(seed), 26)
    part_keys = jax.random.split(jax.random.fold_in(key_of[25], part), 26)
    fine_latent = bell_draw(part_keys[0], (NF, L), 1.0, 6.0, ((0, 16),))
    fine_edges = bell_draw(part_keys[1], (NE, L), 1.0, 6.0, ((0, 16),))
    fine_sender = with_ends(jax.random.randint(part_keys[2], (NE,), 0, NF_DEV + 2 * HS), jax.random.fold_in(part_keys[2], 1), 0, (NF_DEV + 2 * HS) - 1).astype(jnp.int32)
    fine_receiver = draw_fine_receiver(jax.random.fold_in(jax.random.fold_in(key_of[25], part), 71), part)
    edge_count = draw_edge_count(jax.random.fold_in(jax.random.fold_in(key_of[25], part), 71), part)
    fine_border = with_ends(jax.random.randint(part_keys[5], (N_DOM, 2, HS), 0, NF_DEV), jax.random.fold_in(part_keys[5], 1), 0, NF_DEV - 1).astype(jnp.int32)
    pool_rows = with_ends(jax.random.randint(part_keys[6], (N_DOM, 2, CAP), 0, NF_DEV), jax.random.fold_in(part_keys[6], 1), 0, NF_DEV - 1).astype(jnp.int32)
    pool_target = with_ends(jax.random.randint(part_keys[7], (N_DOM, 2, CAP), 0, N1_DEV), jax.random.fold_in(part_keys[7], 1), 0, N1_DEV - 1).astype(jnp.int32)
    pool_weight = draw_pool_weight(jax.random.fold_in(jax.random.fold_in(key_of[25], part), 71), part)
    fine_parent = draw_fine_parent(jax.random.fold_in(jax.random.fold_in(key_of[25], part), 71), part)
    fine_weight = with_ends(jax.random.randint(part_keys[10], (NF,), 1, 5), jax.random.fold_in(part_keys[10], 1), 1, 4).astype(jnp.int32)
    coarse_edges = bell_draw(part_keys[11], (NE1, L), 1.0, 6.0, ((0, 16),))
    coarse_sender = with_ends(jax.random.randint(part_keys[12], (NE1,), 0, N1_DEV + 2 * HS1), jax.random.fold_in(part_keys[12], 1), 0, (N1_DEV + 2 * HS1) - 1).astype(jnp.int32)
    coarse_receiver = draw_coarse_receiver(jax.random.fold_in(jax.random.fold_in(key_of[25], part), 71), part)
    coarse_border = with_ends(jax.random.randint(part_keys[14], (N_DOM, 2, HS1), 0, N1_DEV), jax.random.fold_in(part_keys[14], 1), 0, N1_DEV - 1).astype(jnp.int32)
    coarse_parent = draw_coarse_parent(jax.random.fold_in(jax.random.fold_in(key_of[25], part), 71), part)
    coarse_weight = with_ends(jax.random.randint(part_keys[16], (N1,), 1, 5), jax.random.fold_in(part_keys[16], 1), 1, 4).astype(jnp.int32)
    top_edges = bell_draw(part_keys[17], (NE2, L), 1.0, 6.0)
    top_sender = with_ends(jax.random.randint(part_keys[18], (NE2,), 0, N2), jax.random.fold_in(part_keys[18], 1), 0, N2 - 1).astype(jnp.int32)
    top_receiver = draw_top_receiver(jax.random.fold_in(jax.random.fold_in(key_of[25], part), 71), part)
    edge_in = bell_draw(key_of[20], (LEVELS, 3 * L, L), (3 * L) ** -0.5, 0.3125)
    edge_out = bell_draw(key_of[21], (LEVELS, L, L), L ** -0.5, 0.5)
    node_in = bell_draw(key_of[22], (LEVELS, 2 * L, L), (2 * L) ** -0.5, 0.375)
    node_out = bell_draw(key_of[23], (LEVELS, L, L), L ** -0.5, 0.5)
    norm_gain = jnp.clip(1.0 + 0.18 * jax.random.normal(key_of[24], (LEVELS, 2, L), jnp.float32), 0.1, 1.9)
    return dict(fine_latent=fine_latent, fine_edges=fine_edges, fine_sender=fine_sender, fine_receiver=fine_receiver, edge_count=edge_count, fine_border=fine_border, pool_rows=pool_rows, pool_target=pool_target, pool_weight=pool_weight, fine_parent=fine_parent, fine_weight=fine_weight, coarse_edges=coarse_edges, coarse_sender=coarse_sender, coarse_receiver=coarse_receiver, coarse_border=coarse_border, coarse_parent=coarse_parent, coarse_weight=coarse_weight, top_edges=top_edges, top_sender=top_sender, top_receiver=top_receiver, edge_in=edge_in, edge_out=edge_out, node_in=node_in, node_out=node_out, norm_gain=norm_gain)


epsilon = 1e-05

def layer_norm(values, gain_row):
    row_mean = lax.optimization_barrier(jnp.mean(values, axis=-1, keepdims=True))
    centred = values - row_mean
    spread = lax.optimization_barrier(jnp.mean(centred * centred, axis=-1, keepdims=True))
    return centred * lax.rsqrt(spread + epsilon) * gain_row

def graph_step(node_rows, sender_rows, receiver, edge_rows, live_mask, w_edge_in, w_edge_out, w_node_in, w_node_out, gains):
    joined = jnp.concatenate([sender_rows, node_rows[receiver], edge_rows], axis=1)
    hidden = jax.nn.relu(jnp.dot(joined, w_edge_in, preferred_element_type=jnp.float32)).astype(jnp.bfloat16)
    message = layer_norm(jnp.dot(hidden, w_edge_out, preferred_element_type=jnp.float32), gains[0]) * live_mask[:, None]
    summed = jax.ops.segment_sum(message, receiver, num_segments=node_rows.shape[0]).astype(jnp.bfloat16)
    joined_nodes = jnp.concatenate([node_rows, summed], axis=1)
    inner_rows = jax.nn.relu(jnp.dot(joined_nodes, w_node_in, preferred_element_type=jnp.float32)).astype(jnp.bfloat16)
    update = layer_norm(jnp.dot(inner_rows, w_node_out, preferred_element_type=jnp.float32), gains[1])
    return (node_rows.astype(jnp.float32) + update).astype(jnp.bfloat16)

def select_rows(table, index):
    return table[index]

def ghost_rows(latent, border):
    picker = jax.vmap(select_rows)
    to_left = picker(latent, border[:, 0])
    to_right = picker(latent, border[:, 1])
    blank = jnp.zeros_like(to_left[:1])
    from_left = jnp.concatenate([blank, to_right[:-1]], axis=0)
    from_right = jnp.concatenate([to_left[1:], blank], axis=0)
    return jnp.concatenate([latent, from_left, from_right], axis=1)

def reference(fine_latent, fine_edges, fine_sender, fine_receiver, edge_count, fine_border, pool_rows, pool_target, pool_weight, fine_parent, fine_weight, coarse_edges, coarse_sender, coarse_receiver, coarse_border, coarse_parent, coarse_weight, top_edges, top_sender, top_receiver, edge_in, edge_out, node_in, node_out, norm_gain):
    picker = jax.vmap(select_rows)
    latent = fine_latent.reshape(N_DOM, NF_DEV, L)
    extended = ghost_rows(latent, fine_border)
    positions = jnp.arange(NE_DEV, dtype=jnp.int32)

    def fine_part(pieces):
        node_rows, ext_rows, sender, receiver, edge_rows, live_count = pieces
        live_mask = (positions < live_count).astype(jnp.float32)
        return graph_step(node_rows, ext_rows[sender], receiver, edge_rows, live_mask, edge_in[0], edge_out[0], node_in[0], node_out[0], norm_gain[0])
    fine_new = lax.map(fine_part, (latent, extended, fine_sender.reshape(N_DOM, NE_DEV), fine_receiver.reshape(N_DOM, NE_DEV), fine_edges.reshape(N_DOM, NE_DEV, L), edge_count))
    to_lower = picker(fine_new, pool_rows[:, 0])
    to_upper = picker(fine_new, pool_rows[:, 1])
    blank = jnp.zeros_like(to_lower[:1])
    from_lower = jnp.concatenate([blank, to_upper[:-1]], axis=0)
    from_upper = jnp.concatenate([to_lower[1:], blank], axis=0)
    arrived_rows = jnp.stack([from_lower, from_upper], axis=1).reshape(N_DOM * 2 * CAP, L)
    owners = jnp.arange(N_DOM, dtype=jnp.int32)
    remote_ids = (owners[:, None, None] * N1_DEV + pool_target).reshape(N_DOM * 2 * CAP)
    remote_weight = pool_weight.reshape(N_DOM * 2 * CAP).astype(jnp.float32)
    local_ids = (owners[:, None] * N1_DEV + fine_parent.reshape(N_DOM, NF_DEV)).reshape(N_DOM * NF_DEV)
    local_weight = fine_weight.astype(jnp.float32)
    coarse_count = N_DOM * N1_DEV
    pooled = jax.ops.segment_sum(local_weight[:, None] * fine_new.reshape(N_DOM * NF_DEV, L).astype(jnp.float32), local_ids, num_segments=coarse_count)
    pooled = pooled + jax.ops.segment_sum(remote_weight[:, None] * arrived_rows.astype(jnp.float32), remote_ids, num_segments=coarse_count)
    weight_sum = jax.ops.segment_sum(local_weight, local_ids, num_segments=coarse_count) + jax.ops.segment_sum(remote_weight, remote_ids, num_segments=coarse_count)
    coarse_in = (pooled / weight_sum[:, None]).astype(jnp.bfloat16).reshape(N_DOM, N1_DEV, L)
    coarse_ext = ghost_rows(coarse_in, coarse_border)
    coarse_mask = jnp.ones((NE1_DEV,), jnp.float32)

    def coarse_part(pieces):
        node_rows, ext_rows, sender, receiver, edge_rows = pieces
        return graph_step(node_rows, ext_rows[sender], receiver, edge_rows, coarse_mask, edge_in[1], edge_out[1], node_in[1], node_out[1], norm_gain[1])
    coarse_new = lax.map(coarse_part, (coarse_in, coarse_ext, coarse_sender.reshape(N_DOM, NE1_DEV), coarse_receiver.reshape(N_DOM, NE1_DEV), coarse_edges.reshape(N_DOM, NE1_DEV, L)))
    coarse_new = coarse_new.reshape(N_DOM * N1_DEV, L)
    top_weight = coarse_weight.astype(jnp.float32)
    top_sum = jax.ops.segment_sum(top_weight[:, None] * coarse_new.astype(jnp.float32), coarse_parent, num_segments=N2)
    top_total = jax.ops.segment_sum(top_weight, coarse_parent, num_segments=N2)
    top_in = (top_sum / top_total[:, None]).astype(jnp.bfloat16)
    top_mask = jnp.ones((NE2,), jnp.float32)
    top_new = graph_step(top_in, top_in[top_sender], top_receiver, top_edges, top_mask, edge_in[2], edge_out[2], node_in[2], node_out[2], norm_gain[2])
    coarse_out = (coarse_new.astype(jnp.float32) + top_new[coarse_parent].astype(jnp.float32)).astype(jnp.bfloat16)
    lifted = picker(coarse_out.reshape(N_DOM, N1_DEV, L), fine_parent.reshape(N_DOM, NF_DEV)).reshape(N_DOM * NF_DEV, L)
    fine_out = (fine_new.reshape(N_DOM * NF_DEV, L).astype(jnp.float32) + lifted.astype(jnp.float32)).astype(jnp.bfloat16)
    return (fine_out, coarse_out)
```

```python
import functools

import jax
import jax.numpy as jnp
from jax import lax
from jax.experimental import pallas as pl
from jax.experimental.pallas import tpu as pltpu
from jax.sharding import PartitionSpec as P

epsilon = 1e-05
bf16 = jnp.bfloat16
f32 = jnp.float32
LANES = 128
GROUP = 4
VMEM_LIMIT = 52 * 2**20
whole_vmem = pl.BlockSpec(memory_space=pltpu.VMEM)
whole_smem = pl.BlockSpec(memory_space=pltpu.SMEM)
left_in_hbm = pl.BlockSpec(memory_space=pl.ANY)


def mm(a, b):
    return jnp.dot(a, b, preferred_element_type=f32)


def mm_first(a, b):
    return lax.dot_general(a, b, (((0,), (0,)), ((), ())), preferred_element_type=f32)


def gather_rows(index_ref, first, table_ref, into_ref, count, into_first=0):
    for j in range(count):
        into_ref[pl.ds(into_first + j, 1), :] = table_ref[pl.ds(index_ref[first + j], 1), :]


def match_rows(ids_row, count, weight_row=None):
    shape = (count, ids_row.shape[1])
    hit = lax.broadcasted_iota(jnp.int32, shape, 0) == ids_row
    if weight_row is None:
        return hit.astype(f32).astype(bf16)
    return jnp.where(hit, weight_row, 0.0).astype(bf16)


def side_by_side(rows):
    half = rows.shape[0] // 2
    return jnp.concatenate([rows[:half], rows[half:]], axis=1)


def normed_pairs(hidden, w_centred, spread_of):
    centred = mm(side_by_side(hidden), w_centred)
    spread = mm((centred * centred).astype(bf16), spread_of)
    return centred * lax.rsqrt(spread + epsilon)


def edge_sums(sender_part, receiver_part, edge_rows, picks, w_edge, w_out, spread_of):
    before = mm_first(picks, receiver_part) + mm(edge_rows, w_edge)
    hidden = jnp.maximum(before + sender_part, 0.0).astype(bf16)
    message = normed_pairs(hidden, w_out, spread_of).astype(bf16)
    half = edge_rows.shape[0] // 2
    return mm(picks[:, :half], message[:, :LANES]) + mm(picks[:, half:], message[:, LANES:])


def node_update(node_rows, summed, w_node, w_out, spread_of, gain):
    hidden = jnp.maximum(mm(jnp.concatenate([node_rows, summed], axis=1), w_node), 0.0)
    update = normed_pairs(hidden.astype(bf16), w_out, spread_of)
    update = jnp.concatenate([update[:, :LANES], update[:, LANES:]], axis=0)
    return (node_rows.astype(f32) + update * gain).astype(bf16)


def with_ones(rows):
    return jnp.concatenate([rows, jnp.ones(rows.shape, bf16)], axis=1)


def border_kernel(index_ref, x_ref, a_ref, b_ref, table, buffer):
    table[...] = x_ref[...].astype(f32)
    count = a_ref.shape[0]
    for side, out in enumerate((a_ref, b_ref)):
        gather_rows(index_ref, side * count, table, buffer, count)
        out[...] = buffer[...].astype(bf16)


def fill_tables(x_ref, place_ref, from_a, from_b, w_sr, table, receiver_part):
    count = x_ref.shape[0]
    border = from_a.shape[0]
    both = mm(x_ref[...], w_sr[...])
    table[:count, :] = both[:, :LANES]
    receiver_part[...] = both[:, LANES:].astype(bf16)
    w_s = w_sr[:, :LANES]
    at_a = pl.multiple_of(count + place_ref[0] * border, border)
    at_b = pl.multiple_of(count + (1 - place_ref[0]) * border, border)
    table[pl.ds(at_a, border), :] = mm(from_a[...], w_s)
    table[pl.ds(at_b, border), :] = mm(from_b[...], w_s) * place_ref[1].astype(f32)


def fine_kernel(
    place_ref, pool_index, sender_ref, edge_ref, x_ref, from_a, from_b, receiver_ref, parent_ref,
    weight_ref, w_sr, w_edge, w_out, w_node, w_node_out, spread_ref, gain_ref,
    new_ref, sums_ref, a_ref, b_ref,
    table, receiver_part, edges, gathered0, gathered1, aggregate, new32, buffer,
    index0, index1, index2, index3, edge_sem, index_sem,
):
    gathered = (gathered0, gathered1)
    indices = (index0, index1, index2, index3)
    block = gathered0.shape[0]
    groups, _, group_nodes = parent_ref.shape
    nodes = group_nodes // GROUP
    chunk = GROUP * block

    def edge_copy(g):
        at = pl.ds(pl.multiple_of(g * chunk, chunk), chunk)
        return pltpu.make_async_copy(edge_ref.at[at, :], edges.at[at, :], edge_sem.at[g])

    def index_copy(t, k):
        at = pl.ds(pl.multiple_of(t * block, block), block)
        return pltpu.make_async_copy(sender_ref.at[at], indices[k], index_sem.at[k])

    for k in range(GROUP):
        index_copy(k, k).start()
    for g in range(groups):
        edge_copy(g).start()
    fill_tables(x_ref, place_ref, from_a, from_b, w_sr, table, receiver_part)
    sums_ref[...] = jnp.zeros_like(sums_ref)
    index_copy(0, 0).wait()
    gather_rows(index0, 0, table, gathered0, block)

    def group_step(g, carry):
        edge_copy(g).wait()
        for k in range(GROUP):
            t = g * GROUP + k
            later = (k + 1) % GROUP
            index_copy(t + 1, later).wait()
            index_copy(t + GROUP, k).start()
            gather_rows(indices[later], 0, table, gathered[(k + 1) % 2], block)
            picks = match_rows(receiver_ref[t], nodes)
            summed = edge_sums(
                gathered[k % 2][...],
                receiver_part[pl.ds(pl.multiple_of(t * nodes, nodes), nodes), :],
                edges[pl.ds(pl.multiple_of(t * block, block), block), :],
                picks, w_edge[...], w_out[...], spread_ref[...],
            )
            aggregate[k * nodes : (k + 1) * nodes, :] = (summed * gain_ref[0:1, :]).astype(bf16)
        rows = pl.ds(pl.multiple_of(g * group_nodes, group_nodes), group_nodes)
        new_rows = node_update(
            x_ref[rows, :], aggregate[...], w_node[...], w_node_out[...], spread_ref[...],
            gain_ref[1:2, :],
        )
        new_ref[rows, :] = new_rows
        new32[rows, :] = new_rows.astype(f32)
        shares = match_rows(parent_ref[g], sums_ref.shape[0], weight_ref[g])
        sums_ref[...] += mm(shares, with_ones(new_rows))
        return carry

    lax.fori_loop(0, groups, group_step, 0)
    for k in range(1, GROUP):
        index_copy(groups * GROUP + k, k).wait()
    count = a_ref.shape[0]
    for side, out in enumerate((a_ref, b_ref)):
        gather_rows(pool_index, side * count, new32, buffer, count)
        out[...] = buffer[...].astype(bf16)


def pool_kernel(
    border_index, sums_ref, from_a, from_b, target_ref, weight_ref, coarse_ref, a_ref, b_ref, table, buffer
):
    count = sums_ref.shape[0]
    total = sums_ref[...]
    for side, rows in enumerate((from_a, from_b)):
        shares = match_rows(target_ref[side], count, weight_ref[side])
        total += mm(shares, with_ones(rows[...]))
    coarse = (total[:, :LANES] / total[:, LANES:]).astype(bf16)
    coarse_ref[...] = coarse
    table[...] = coarse.astype(f32)
    border = a_ref.shape[0]
    for side, out in enumerate((a_ref, b_ref)):
        gather_rows(border_index, side * border, table, buffer, border)
        out[...] = buffer[...].astype(bf16)


def coarse_kernel(
    place_ref, sender_ref, edge_ref, x_ref, from_a, from_b, receiver_ref, parent_ref, weight_ref,
    w_sr, w_edge, w_out, w_node, w_node_out, spread_ref, gain_ref,
    new_ref, own_ref, a_ref, b_ref,
    table, receiver_part, gathered, aggregate, shares_sum,
):
    blocks, _, block = receiver_ref.shape
    nodes = x_ref.shape[0] // blocks
    fill_tables(x_ref, place_ref, from_a, from_b, w_sr, table, receiver_part)
    for t in range(blocks):
        gather_rows(sender_ref, t * block, table, gathered, block, t * block)
    for t in range(blocks):
        picks = match_rows(receiver_ref[t], nodes)
        summed = edge_sums(
            gathered[t * block : (t + 1) * block, :],
            receiver_part[t * nodes : (t + 1) * nodes, :],
            edge_ref[t * block : (t + 1) * block, :],
            picks, w_edge[...], w_out[...], spread_ref[...],
        )
        aggregate[t * nodes : (t + 1) * nodes, :] = (summed * gain_ref[0:1, :]).astype(bf16)
    new_rows = node_update(
        x_ref[...], aggregate[...], w_node[...], w_node_out[...], spread_ref[...], gain_ref[1:2, :]
    )
    new_ref[...] = new_rows
    share = own_ref.shape[0]
    shares_sum[...] = mm(match_rows(parent_ref[...], 3 * share, weight_ref[...]), with_ones(new_rows))
    own_ref[...] = shares_sum[share : 2 * share, :]
    a_ref[...] = shares_sum[pl.ds(pl.multiple_of(2 * share * place_ref[0], share), share), :]
    b_ref[...] = shares_sum[pl.ds(pl.multiple_of(2 * share * (1 - place_ref[0]), share), share), :]


def top_kernel(
    place_ref, sender_ref, up_index, edge_ref, gathered_in, receiver_ref, parent_ref, coarse_ref,
    fine_ref, w_sr, w_edge, w_out, w_node, w_node_out, spread_ref, gain_ref,
    fine_out, coarse_out,
    table, top_rows, gathered, coarse32, lifted,
):
    share = receiver_ref.shape[1] // 6
    parts = gathered_in.shape[0] // share
    me = place_ref[0]
    nodes = 3 * share
    sender_part = mm(gathered_in[...], w_sr[:, :LANES])
    for q in range(parts):
        at = pl.multiple_of((q ^ me) * share, share)
        table[pl.ds(at, share), :] = sender_part[q * share : (q + 1) * share, :]
        top_rows[pl.ds(at, share), :] = gathered_in[q * share : (q + 1) * share, :]
    window = top_rows[pl.ds(pl.multiple_of(place_ref[1] * share, share), nodes), :]
    block = gathered.shape[0]
    gather_rows(sender_ref, 0, table, gathered, block)
    picks = match_rows(receiver_ref[...], nodes)
    summed = edge_sums(
        gathered[...], mm(window, w_sr[:, LANES:]).astype(bf16), edge_ref[...],
        picks, w_edge[...], w_out[...], spread_ref[...],
    )
    top_new = node_update(
        window, (summed * gain_ref[0:1, :]).astype(bf16), w_node[...], w_node_out[...],
        spread_ref[...], gain_ref[1:2, :],
    )
    up = mm_first(match_rows(parent_ref[...], nodes), top_new)
    coarse = (coarse_ref[...].astype(f32) + up).astype(bf16)
    coarse_out[...] = coarse
    coarse32[...] = coarse.astype(f32)
    step = lifted.shape[0]

    def lift(i, carry):
        gather_rows(up_index, i * step, coarse32, lifted, step)
        rows = pl.ds(pl.multiple_of(i * step, step), step)
        fine_out[rows, :] = (fine_ref[rows, :].astype(f32) + lifted[...]).astype(bf16)
        return carry

    lax.fori_loop(0, fine_ref.shape[0] // step, lift, 0)


def call(kernel, name, outs, specs, scratch, operands):
    return pl.pallas_call(
        kernel,
        name=name,
        out_shape=outs,
        in_specs=specs,
        out_specs=jax.tree.map(lambda _: whole_vmem, outs),
        scratch_shapes=scratch,
        compiler_params=pltpu.CompilerParams(vmem_limit_bytes=VMEM_LIMIT),
    )(*operands)


def rows_of(count, dtype=bf16, width=LANES):
    return jax.ShapeDtypeStruct((count, width), dtype)


def swap_with_neighbours(for_a, for_b):
    count = lax.axis_size("dom")
    pairs_a = [(i, i ^ 1) for i in range(count)]
    pairs_b = [(i, (i + 1) % count) for i in range(1, count, 2)]
    pairs_b += [(j, i) for i, j in pairs_b]
    return lax.ppermute(for_a, "dom", pairs_a), lax.ppermute(for_b, "dom", pairs_b)


def gather_all(rows):
    count = lax.axis_size("dom")
    steps = []
    stride = 1
    while stride < count:
        radix = 4 if stride * 4 <= count else 2
        steps.append((stride, radix))
        stride *= radix
    blocks = rows[None]
    for stride, radix in reversed(steps):
        taken = [blocks] + [
            lax.ppermute(blocks, "dom", [(i, i ^ (j * stride)) for i in range(count)])
            for j in range(1, radix)
        ]
        blocks = jnp.stack(taken, axis=1).reshape((-1,) + rows.shape)
    return blocks


def centred_pairs(weights):
    wide = weights.astype(f32)
    centred = (wide - jnp.mean(wide, axis=2, keepdims=True)).astype(bf16)
    blank = jnp.zeros_like(centred)
    return jnp.concatenate(
        [jnp.concatenate([centred, blank], axis=2), jnp.concatenate([blank, centred], axis=2)], axis=1
    )


def body(
    fine_latent, fine_edges, fine_sender, fine_receiver, edge_count, fine_border, pool_rows, pool_target,
    pool_weight, fine_parent, fine_weight, coarse_edges, coarse_sender, coarse_receiver, coarse_border,
    coarse_parent, coarse_weight, top_edges, top_sender, top_receiver, edge_in, edge_out, node_in, node_out,
    norm_gain,
):
    count = lax.axis_size("dom")
    me = lax.axis_index("dom").astype(jnp.int32)
    odd = me % 2
    inner = jnp.where((me == 0) | (me == count - 1), 0, 1).astype(jnp.int32)
    place = jnp.stack([1 - odd, inner])

    def by_partner(pair):
        return jnp.where(odd == 1, pair, pair[::-1])

    w_sr = jnp.concatenate([edge_in[:, :LANES], edge_in[:, LANES : 2 * LANES]], axis=2)
    w_edge = edge_in[:, 2 * LANES :]
    w_out = centred_pairs(edge_out)
    w_node_out = centred_pairs(node_out)
    lane = jnp.arange(2 * LANES, dtype=jnp.int32) // LANES
    spread_of = jnp.where(lane[:, None] == lane[None, :], 1.0 / LANES, 0.0).astype(bf16)

    def weights_of(level):
        return (
            w_sr[level], w_edge[level], w_out[level], node_in[level], w_node_out[level], spread_of,
            norm_gain[level],
        )

    fine_total = fine_latent.shape[0]
    edge_total = fine_sender.shape[0]
    coarse_total = coarse_parent.shape[0]
    border = fine_border.shape[2]
    slots = pool_rows.shape[2]

    with jax.named_scope("fine_border_rows"):
        for_a, for_b = call(
            border_kernel, "border_rows", [rows_of(border), rows_of(border)], [whole_smem, whole_vmem],
            [pltpu.VMEM((fine_total, LANES), f32), pltpu.VMEM((border, LANES), f32)],
            (by_partner(fine_border[0]).reshape(-1), fine_latent),
        )
        from_a, from_b = swap_with_neighbours(for_a, for_b)

    with jax.named_scope("fine_step"):
        nodes = LANES
        block = nodes * edge_total // fine_total
        blocks = edge_total // block
        groups = blocks // GROUP
        slot = jnp.arange(edge_total, dtype=jnp.int32)
        receiver = jnp.where(slot < edge_count[0], fine_receiver - slot // block * nodes, -1)
        sender = jnp.concatenate([fine_sender, jnp.zeros((GROUP * block,), jnp.int32)])
        fine_new, local_sums, for_a, for_b = call(
            fine_kernel, "fine_step",
            [rows_of(fine_total), rows_of(coarse_total, f32, 2 * LANES), rows_of(slots), rows_of(slots)],
            [whole_smem, whole_smem, left_in_hbm, left_in_hbm] + [whole_vmem] * 13,
            [
                pltpu.VMEM((fine_total + 2 * border, LANES), f32),
                pltpu.VMEM((fine_total, LANES), bf16),
                pltpu.VMEM((edge_total, LANES), bf16),
                pltpu.VMEM((block, LANES), f32),
                pltpu.VMEM((block, LANES), f32),
                pltpu.VMEM((GROUP * nodes, LANES), bf16),
                pltpu.VMEM((fine_total, LANES), f32),
                pltpu.VMEM((slots, LANES), f32),
            ]
            + [pltpu.SMEM((block,), jnp.int32)] * GROUP
            + [pltpu.SemaphoreType.DMA((groups,)), pltpu.SemaphoreType.DMA((GROUP,))],
            (
                place, by_partner(pool_rows[0]).reshape(-1), sender, fine_edges, fine_latent, from_a, from_b,
                receiver.reshape(blocks, 1, block), fine_parent.reshape(groups, 1, GROUP * nodes),
                fine_weight.astype(f32).reshape(groups, 1, GROUP * nodes),
            )
            + weights_of(0),
        )
        from_a, from_b = swap_with_neighbours(for_a, for_b)

    with jax.named_scope("coarse_input"):
        border1 = coarse_border.shape[2]
        coarse_in, for_a, for_b = call(
            pool_kernel, "coarse_input",
            [rows_of(coarse_total), rows_of(border1), rows_of(border1)],
            [whole_smem] + [whole_vmem] * 5,
            [pltpu.VMEM((coarse_total, LANES), f32), pltpu.VMEM((border1, LANES), f32)],
            (
                by_partner(coarse_border[0]).reshape(-1), local_sums, from_a, from_b,
                by_partner(pool_target[0])[:, None, :], by_partner(pool_weight[0]).astype(f32)[:, None, :],
            ),
        )
        from_a, from_b = swap_with_neighbours(for_a, for_b)

    with jax.named_scope("coarse_step"):
        edge_total1 = coarse_sender.shape[0]
        block1 = LANES * edge_total1 // coarse_total
        blocks1 = edge_total1 // block1
        share = coarse_total // 8
        slot1 = jnp.arange(edge_total1, dtype=jnp.int32)
        coarse_new, own, for_a, for_b = call(
            coarse_kernel, "coarse_step",
            [rows_of(coarse_total)] + [rows_of(share, f32, 2 * LANES)] * 3,
            [whole_smem, whole_smem] + [whole_vmem] * 14,
            [
                pltpu.VMEM((coarse_total + 2 * border1, LANES), f32),
                pltpu.VMEM((coarse_total, LANES), bf16),
                pltpu.VMEM((edge_total1, LANES), f32),
                pltpu.VMEM((coarse_total, LANES), bf16),
                pltpu.VMEM((3 * share, 2 * LANES), f32),
            ],
            (
                place, coarse_sender, coarse_edges, coarse_in, from_a, from_b,
                (coarse_receiver - slot1 // block1 * LANES).reshape(blocks1, 1, block1),
                (coarse_parent - (me - 1) * share)[None, :], coarse_weight.astype(f32)[None, :],
            )
            + weights_of(1),
        )
        from_a, from_b = swap_with_neighbours(for_a, for_b)
        shares = own + from_a + from_b
        top_in = (shares[:, :LANES] / shares[:, LANES:]).astype(bf16)

    with jax.named_scope("top_step"):
        everyone = gather_all(top_in).reshape(count * share, LANES)
        first = jnp.clip(me - 1, 0, count - 3)
        tile = 2 * share
        window = 3 * tile
        top_window = [
            lax.dynamic_slice_in_dim(a, first * tile, window, axis=0)
            for a in (top_edges, top_sender, top_receiver)
        ]
        step = 512
        fine_out, coarse_out = call(
            top_kernel, "top_step",
            [rows_of(fine_total), rows_of(coarse_total)],
            [whole_smem] * 3 + [whole_vmem] * 13,
            [
                pltpu.VMEM((count * share, LANES), f32),
                pltpu.VMEM((count * share, LANES), bf16),
                pltpu.VMEM((window, LANES), f32),
                pltpu.VMEM((coarse_total, LANES), f32),
                pltpu.VMEM((step, LANES), f32),
            ],
            (
                jnp.stack([me, first]), top_window[1], fine_parent, top_window[0], everyone,
                (top_window[2] - first * share)[None, :], (coarse_parent - first * share)[None, :], coarse_new,
                fine_new,
            )
            + weights_of(2),
        )
    return (fine_out, coarse_out)


def solution(mesh):
    row = ("groups", "dom")
    return jax.shard_map(
        body,
        mesh=mesh,
        in_specs=(
            P(row, None), P(row, None), P(row), P(row), P(row), P(row, None, None), P(row, None, None),
            P(row, None, None), P(row, None, None), P(row), P(row), P(row, None), P(row), P(row),
            P(row, None, None), P(row), P(row), P("groups", None), P("groups"), P("groups"), P(), P(), P(), P(),
            P(),
        ),
        out_specs=(P(row, None), P(row, None)),
        check_vma=False,
    )
```

```python
import functools

import jax
import jax.numpy as jnp
from jax import lax
from jax.experimental import pallas as pl
from jax.experimental.pallas import tpu as pltpu
from jax.sharding import PartitionSpec as P

epsilon = 1e-05
bf16 = jnp.bfloat16
f32 = jnp.float32
LANES = 128
GROUP = 4
SPLIT = (64, 192, 256, 384)
VMEM_LIMIT = 52 * 2**20
whole_vmem = pl.BlockSpec(memory_space=pltpu.VMEM)
whole_smem = pl.BlockSpec(memory_space=pltpu.SMEM)
left_in_hbm = pl.BlockSpec(memory_space=pl.ANY)


def mm(a, b):
    return jnp.dot(a, b, preferred_element_type=f32)


def mm_first(a, b):
    return lax.dot_general(a, b, (((0,), (0,)), ((), ())), preferred_element_type=f32)


def gather_rows(index, table_ref, into_ref, count, into_first=0):
    for j in range(count):
        into_ref[pl.ds(into_first + j, 1), :] = table_ref[pl.ds(index(j), 1), :]


def match_rows(ids_row, count, weight_row=None):
    shape = (count, ids_row.shape[1])
    hit = lax.broadcasted_iota(jnp.int32, shape, 0) == ids_row
    if weight_row is None:
        return hit.astype(f32).astype(bf16)
    return jnp.where(hit, weight_row.astype(f32), 0.0).astype(bf16)


def aligned(at, size):
    return pl.ds(pl.multiple_of(at, size), size)


def side_by_side(rows):
    half = rows.shape[0] // 2
    return jnp.concatenate([rows[:half], rows[half:]], axis=1)


def normed_pairs(pairs, w_centred, spread_of):
    centred = mm(pairs, w_centred)
    spread = mm((centred * centred).astype(bf16), spread_of)
    return centred * lax.rsqrt(spread + epsilon)


def with_ones(rows):
    return jnp.concatenate([rows, jnp.ones(rows.shape, bf16)], axis=1)


def fill_weights(edge_out, node_out, w_out, w_node_out, spread_of):
    for weights, into in ((edge_out, w_out), (node_out, w_node_out)):
        wide = weights[...].astype(f32)
        centred = (wide - jnp.mean(wide, axis=1, keepdims=True)).astype(bf16)
        into[...] = jnp.zeros_like(into)
        into[:LANES, :LANES] = centred
        into[LANES:, LANES:] = centred
    shape = spread_of.shape
    same = (lax.broadcasted_iota(jnp.int32, shape, 0) < LANES) == (lax.broadcasted_iota(jnp.int32, shape, 1) < LANES)
    spread_of[...] = jnp.where(same, 1.0 / LANES, 0.0).astype(bf16)


weight_scratch = [pltpu.VMEM((2 * LANES, 2 * LANES), bf16)] * 3


weight_specs = [whole_vmem] * 5


def at_level(kernel, level, first):
    def with_level(*refs):
        one = [ref.at[level] for ref in refs[first : first + len(weight_specs)]]
        kernel(*refs[:first], *one, *refs[first + len(weight_specs) :])

    return with_level


def edge_first(picks, receiver_part, edge_rows, sender_part, w_edge):
    before = mm_first(picks, receiver_part) + mm(edge_rows, w_edge)
    return side_by_side(jnp.maximum(before + sender_part, 0.0).astype(bf16))


def edge_sums(picks, message, gain):
    half = picks.shape[1] // 2
    summed = mm(picks[:, :half], message[:, :LANES]) + mm(picks[:, half:], message[:, LANES:])
    return (summed * gain).astype(bf16)


def node_first(node_rows, summed, w_node):
    hidden = mm(jnp.concatenate([node_rows, summed], axis=1), w_node)
    return side_by_side(jnp.maximum(hidden, 0.0).astype(bf16))


def node_last(node_rows, update, gain):
    update = jnp.concatenate([update[:, :LANES], update[:, LANES:]], axis=0)
    return (node_rows.astype(f32) + update * gain).astype(bf16)


def border_kernel(place_ref, index_ref, x_ref, a_ref, b_ref, table, buffer):
    table[...] = x_ref[...].astype(f32)
    count = a_ref.shape[0]
    for side in range(2):
        gather_rows(lambda j: index_ref[0, side, j], table, buffer, count, side * count)
    a_ref[...] = buffer[aligned(count * place_ref[0], count), :].astype(bf16)
    b_ref[...] = buffer[aligned(count * (1 - place_ref[0]), count), :].astype(bf16)


def fill_tables(x_ref, place_ref, from_a, from_b, edge_in, table, receiver_part):
    count = x_ref.shape[0]
    border = from_a.shape[0]
    both = mm(x_ref[...], jnp.concatenate([edge_in[:LANES, :], edge_in[LANES : 2 * LANES, :]], axis=1))
    table[:count, :] = both[:, :LANES]
    receiver_part[...] = both[:, LANES:].astype(bf16)
    w_s = edge_in[:LANES, :]
    table[aligned(count + place_ref[0] * border, border), :] = mm(from_a[...], w_s)
    table[aligned(count + (1 - place_ref[0]) * border, border), :] = mm(from_b[...], w_s) * place_ref[1].astype(f32)


def fine_kernel(
    place_ref, pool_index, sender_ref, edge_ref, x_ref, from_a, from_b, receiver_ref, parent_ref,
    weight_ref, edge_in, edge_out, node_in, node_out, gain_ref,
    new_ref, sums_ref, a_ref, b_ref,
    table, receiver_part, edges, new32, buffer, aggregate, node_hidden,
    gathered0, gathered1, hidden0, hidden1, message0, message1,
    index0, index1, index2, index3, edge_sem, index_sem, w_out, w_node_out, spread_of,
):
    gathered, hidden, message = (gathered0, gathered1), (hidden0, hidden1), (message0, message1)
    indices = (index0, index1, index2, index3)
    block = gathered0.shape[0]
    groups, _, group_nodes = parent_ref.shape
    nodes = group_nodes // GROUP
    blocks = groups * GROUP
    chunk = GROUP * block
    gain, node_gain = gain_ref[0:1, :], gain_ref[1:2, :]

    def edge_copy(g):
        at = aligned(g * chunk, chunk)
        return pltpu.make_async_copy(edge_ref.at[at, :], edges.at[at, :], edge_sem.at[g])

    def index_copy(t, k):
        at = aligned(jnp.minimum(t, blocks - 1) * block, block)
        return pltpu.make_async_copy(sender_ref.at[at], indices[k], index_sem.at[k])

    def gather_block(k, into):
        gather_rows(lambda j: indices[k][j], table, into, block)

    for k in range(GROUP):
        index_copy(k, k).start()
    for g in range(groups):
        edge_copy(g).start()
    fill_weights(edge_out, node_out, w_out, w_node_out, spread_of)
    fill_tables(x_ref, place_ref, from_a, from_b, edge_in, table, receiver_part)
    sums_ref[...] = jnp.zeros_like(sums_ref)
    index_copy(0, 0).wait()
    gather_block(0, gathered0)

    def picks_of(t):
        t = jnp.maximum(t, 0)
        slot = lax.broadcasted_iota(jnp.int32, (1, block), 1) + t * block
        return match_rows(jnp.where(slot < place_ref[2], receiver_ref[t] - t * nodes, -1), nodes)

    def group_step(g, last):
        if not last:
            edge_copy(g).wait()
        for k in range(GROUP):
            t = g * GROUP + k
            here, before = k % 2, (k + 1) % 2
            if not last:
                later = (k + 1) % GROUP
                index_copy(t + 1, later).wait()
                index_copy(t + GROUP, k).start()
            keep = {}
            done = jnp.maximum(g - 1, 0)
            rows = aligned(done * group_nodes, group_nodes)

            def pick():
                if not last:
                    keep["picks"] = picks_of(t)
                if not last or k < 2:
                    keep["earlier"] = picks_of(t - 2)

            def multiply_first():
                if not last:
                    keep["before"] = mm_first(
                        keep["picks"], receiver_part[aligned(t * nodes, nodes), :]
                    ) + mm(edges[aligned(t * block, block), :], edge_in[2 * LANES :, :])
                if not last or k < 1:
                    keep["centred"] = mm(hidden[before][...], w_out[...])
                if k == 2:
                    node_hidden[...] = node_first(x_ref[rows, :], aggregate[...], node_in[...])
                if k == 3:
                    keep["node_centred"] = mm(node_hidden[...], w_node_out[...])

            def rectify():
                if not last:
                    rows = jnp.maximum(keep["before"] + gathered[here][...], 0.0)
                    hidden[here][...] = side_by_side(rows.astype(bf16))
                if not last or k < 1:
                    keep["squares"] = (keep["centred"] * keep["centred"]).astype(bf16)
                if k == 3:
                    keep["node_squares"] = (keep["node_centred"] * keep["node_centred"]).astype(bf16)

            def multiply_last():
                if not last or k < 1:
                    keep["spread"] = mm(keep["squares"], spread_of[...])
                if not last or k < 2:
                    into = (k - 2) % GROUP * nodes
                    aggregate[into : into + nodes, :] = edge_sums(keep["earlier"], message[here][...], gain)
                if k == 3:
                    keep["node_spread"] = mm(keep["node_squares"], spread_of[...])

            def scale():
                if not last or k < 1:
                    message[before][...] = (keep["centred"] * lax.rsqrt(keep["spread"] + epsilon)).astype(bf16)
                if k == 3:
                    update = keep["node_centred"] * lax.rsqrt(keep["node_spread"] + epsilon)
                    new_rows = node_last(x_ref[rows, :], update, node_gain)
                    new_ref[rows, :] = new_rows
                    new32[rows, :] = new_rows.astype(f32)
                    shares = match_rows(parent_ref[done], sums_ref.shape[0], weight_ref[done])
                    sums = sums_ref[...] + mm(shares, with_ones(new_rows))
                    sums_ref[...] = sums if last else jnp.where(g > 0, sums, 0.0)

            cuts = (0, *SPLIT, block)
            for i, step in enumerate((pick, multiply_first, rectify, multiply_last, scale)):
                step()
                if not last:
                    gather_rows(
                        lambda j: indices[later][cuts[i] + j], table, gathered[before],
                        cuts[i + 1] - cuts[i], cuts[i],
                    )
    def loop_step(g, carry):
        group_step(g, False)
        return carry

    lax.fori_loop(0, groups, loop_step, 0)
    group_step(groups, True)
    for k in range(1, GROUP):
        index_copy(blocks + k, k).wait()
    count = a_ref.shape[0]
    for side in range(2):
        gather_rows(lambda j: pool_index[0, side, j], new32, buffer, count, side * count)
    a_ref[...] = buffer[aligned(count * place_ref[0], count), :].astype(bf16)
    b_ref[...] = buffer[aligned(count * (1 - place_ref[0]), count), :].astype(bf16)


def pool_kernel(
    place_ref, border_index, sums_ref, from_a, from_b, target_ref, weight_ref,
    coarse_ref, a_ref, b_ref, table, buffer,
):
    count = sums_ref.shape[0]
    total = sums_ref[...]
    for side, rows in ((place_ref[0], from_a), (1 - place_ref[0], from_b)):
        shares = match_rows(target_ref[side], count, weight_ref[side])
        total += mm(shares, with_ones(rows[...]))
    coarse = (total[:, :LANES] / total[:, LANES:]).astype(bf16)
    coarse_ref[...] = coarse
    table[...] = coarse.astype(f32)
    border = a_ref.shape[0]
    for side in range(2):
        gather_rows(lambda j: border_index[0, side, j], table, buffer, border, side * border)
    a_ref[...] = buffer[aligned(border * place_ref[0], border), :].astype(bf16)
    b_ref[...] = buffer[aligned(border * (1 - place_ref[0]), border), :].astype(bf16)


def coarse_kernel(
    place_ref, sender_ref, edge_ref, x_ref, from_a, from_b, receiver_ref, parent_ref, weight_ref,
    edge_in, edge_out, node_in, node_out, gain_ref,
    new_ref, own_ref, a_ref, b_ref,
    table, receiver_part, gathered, aggregate, shares_sum, w_out, w_node_out, spread_of,
):
    blocks, _, block = receiver_ref.shape
    nodes = x_ref.shape[0] // blocks
    fill_weights(edge_out, node_out, w_out, w_node_out, spread_of)
    fill_tables(x_ref, place_ref, from_a, from_b, edge_in, table, receiver_part)
    gather_rows(lambda j: sender_ref[j], table, gathered, blocks * block)
    for t in range(blocks):
        at = slice(t * block, (t + 1) * block)
        own = slice(t * nodes, (t + 1) * nodes)
        picks = match_rows(receiver_ref[t] - t * nodes, nodes)
        pairs = edge_first(
            picks, receiver_part[own, :], edge_ref[at, :], gathered[at, :], edge_in[2 * LANES :, :]
        )
        message = normed_pairs(pairs, w_out[...], spread_of[...]).astype(bf16)
        aggregate[own, :] = edge_sums(picks, message, gain_ref[0:1, :])
    pairs = node_first(x_ref[...], aggregate[...], node_in[...])
    new_rows = node_last(x_ref[...], normed_pairs(pairs, w_node_out[...], spread_of[...]), gain_ref[1:2, :])
    new_ref[...] = new_rows
    share = own_ref.shape[0]
    shares = match_rows(parent_ref[...] - (place_ref[3] - 1) * share, 3 * share, weight_ref[...])
    shares_sum[...] = mm(shares, with_ones(new_rows))
    own_ref[...] = shares_sum[share : 2 * share, :]
    a_ref[...] = shares_sum[aligned(2 * share * place_ref[0], share), :]
    b_ref[...] = shares_sum[aligned(2 * share * (1 - place_ref[0]), share), :]


def lift_kernel(parent_ref, picks_ref):
    groups, _, size = parent_ref.shape
    for g in range(groups):
        picks_ref[g * size : (g + 1) * size, :] = match_rows(parent_ref[g], picks_ref.shape[1]).T


def top_kernel(
    place_ref, sender_ref, picks_ref, edge_ref, gathered_in, receiver_ref, parent_ref, coarse_ref,
    fine_ref, edge_in, edge_out, node_in, node_out, gain_ref,
    fine_out, coarse_out,
    picks, table, top_rows, gathered, picks_sem, w_out, w_node_out, spread_of,
):
    chunk = coarse_ref.shape[0]
    chunks = fine_ref.shape[0] // chunk

    def picks_copy(i):
        at = slice(i * chunk, (i + 1) * chunk)
        return pltpu.make_async_copy(picks_ref.at[at, :], picks.at[at, :], picks_sem.at[i])

    for i in range(chunks):
        picks_copy(i).start()
    tile = receiver_ref.shape[2]
    share = tile // 2
    nodes = 3 * share
    block = 3 * tile
    parts = gathered_in.shape[0] // share
    me, first = place_ref[3], place_ref[4]
    fill_weights(edge_out, node_out, w_out, w_node_out, spread_of)
    sender_part = mm(gathered_in[...], edge_in[:LANES, :])
    for q in range(parts):
        at = aligned((q ^ me) * share, share)
        table[at, :] = sender_part[q * share : (q + 1) * share, :]
        top_rows[at, :] = gathered_in[q * share : (q + 1) * share, :]
    window = top_rows[pl.ds(pl.multiple_of(first * share, share), nodes), :]
    gather_rows(lambda j: sender_ref[first * tile + j], table, gathered, block)
    ids = jnp.concatenate([receiver_ref[first + i] for i in range(3)], axis=1) - first * share
    matches = match_rows(ids, nodes)
    pairs = edge_first(
        matches, mm(window, edge_in[LANES : 2 * LANES, :]).astype(bf16),
        edge_ref[pl.ds(pl.multiple_of(first * tile, tile), block), :], gathered[...], edge_in[2 * LANES :, :],
    )
    message = normed_pairs(pairs, w_out[...], spread_of[...]).astype(bf16)
    pairs = node_first(window, edge_sums(matches, message, gain_ref[0:1, :]), node_in[...])
    top_new = node_last(window, normed_pairs(pairs, w_node_out[...], spread_of[...]), gain_ref[1:2, :])
    up = mm_first(match_rows(parent_ref[...] - first * share, nodes), top_new)
    coarse = (coarse_ref[...].astype(f32) + up).astype(bf16)
    coarse_out[...] = coarse
    for i in range(chunks):
        picks_copy(i).wait()
        at = slice(i * chunk, (i + 1) * chunk)
        fine_out[at, :] = (fine_ref[at, :].astype(f32) + mm(picks[at, :], coarse)).astype(bf16)


def call(kernel, name, outs, specs, scratch, operands, flops=0, moved=0):
    return pl.pallas_call(
        kernel,
        name=name,
        out_shape=outs,
        in_specs=specs,
        out_specs=jax.tree.map(lambda _: whole_vmem, outs),
        scratch_shapes=scratch,
        cost_estimate=pl.CostEstimate(flops=flops, bytes_accessed=moved, transcendentals=0),
        compiler_params=pltpu.CompilerParams(vmem_limit_bytes=VMEM_LIMIT),
    )(*operands)


def rows_of(count, dtype=bf16, width=LANES):
    return jax.ShapeDtypeStruct((count, width), dtype)


def swap_with_neighbours(for_a, for_b):
    count = lax.axis_size("dom")
    pairs_a = [(i, i ^ 1) for i in range(count)]
    pairs_b = [(i, (i + 1) % count) for i in range(1, count, 2)]
    pairs_b += [(j, i) for i, j in pairs_b]
    return lax.ppermute(for_a, "dom", pairs_a), lax.ppermute(for_b, "dom", pairs_b)


def gather_all(rows):
    count = lax.axis_size("dom")
    steps = []
    stride = 1
    while stride < count:
        radix = 4 if stride * 4 <= count else 2
        steps.append((stride, radix))
        stride *= radix
    blocks = rows[None]
    for stride, radix in reversed(steps):
        taken = [blocks] + [
            lax.ppermute(blocks, "dom", [(i, i ^ (j * stride)) for i in range(count)])
            for j in range(1, radix)
        ]
        blocks = jnp.stack(taken, axis=1).reshape((-1,) + rows.shape)
    return blocks


def body(
    fine_latent, fine_edges, fine_sender, fine_receiver, edge_count, fine_border, pool_rows, pool_target,
    pool_weight, fine_parent, fine_weight, coarse_edges, coarse_sender, coarse_receiver, coarse_border,
    coarse_parent, coarse_weight, top_edges, top_sender, top_receiver, edge_in, edge_out, node_in, node_out,
    norm_gain,
):
    count = lax.axis_size("dom")
    me = lax.axis_index("dom").astype(jnp.int32)
    inner = jnp.where((me == 0) | (me == count - 1), 0, 1).astype(jnp.int32)
    place = jnp.stack([1 - me % 2, inner, edge_count[0], me, jnp.clip(me - 1, 0, count - 3)])
    weights = (edge_in, edge_out, node_in, node_out, norm_gain)

    fine_total = fine_latent.shape[0]
    edge_total = fine_sender.shape[0]
    coarse_total = coarse_parent.shape[0]
    border = fine_border.shape[2]
    slots = pool_rows.shape[2]
    nodes = LANES
    block = nodes * edge_total // fine_total
    blocks = edge_total // block
    groups = blocks // GROUP

    with jax.named_scope("fine_border_rows"):
        for_a, for_b = call(
            border_kernel, "border_rows", [rows_of(border), rows_of(border)],
            [whole_smem, whole_smem, whole_vmem],
            [pltpu.VMEM((fine_total, LANES), f32), pltpu.VMEM((2 * border, LANES), f32)],
            (place, fine_border, fine_latent),
        )
        from_a, from_b = swap_with_neighbours(for_a, for_b)
        lift_picks = call(
            lift_kernel, "lift_picks", rows_of(fine_total, bf16, coarse_total), [whole_vmem], [],
            (fine_parent.reshape(fine_total // coarse_total, 1, coarse_total),),
            flops=10**9, moved=fine_total * coarse_total * 2,
        )

    with jax.named_scope("fine_step"):
        fine_new, local_sums, for_a, for_b = call(
            at_level(fine_kernel, 0, 10), "fine_step",
            [rows_of(fine_total), rows_of(coarse_total, f32, 2 * LANES), rows_of(slots), rows_of(slots)],
            [whole_smem, whole_smem, left_in_hbm, left_in_hbm] + [whole_vmem] * 6 + weight_specs,
            [
                pltpu.VMEM((fine_total + 2 * border, LANES), f32),
                pltpu.VMEM((fine_total, LANES), bf16),
                pltpu.VMEM((edge_total, LANES), bf16),
                pltpu.VMEM((fine_total, LANES), f32),
                pltpu.VMEM((2 * slots, LANES), f32),
                pltpu.VMEM((GROUP * nodes, LANES), bf16),
                pltpu.VMEM((GROUP * nodes // 2, 2 * LANES), bf16),
            ]
            + [pltpu.VMEM((block, LANES), f32)] * 2
            + [pltpu.VMEM((block // 2, 2 * LANES), bf16)] * 4
            + [pltpu.SMEM((block,), jnp.int32)] * GROUP
            + [pltpu.SemaphoreType.DMA((groups,)), pltpu.SemaphoreType.DMA((GROUP,))]
            + weight_scratch,
            (
                place, pool_rows, fine_sender, fine_edges, fine_latent, from_a, from_b,
                fine_receiver.reshape(blocks, 1, block), fine_parent.reshape(groups, 1, GROUP * nodes),
                fine_weight.reshape(groups, 1, GROUP * nodes),
            )
            + weights,
        )
        from_a, from_b = swap_with_neighbours(for_a, for_b)

    with jax.named_scope("coarse_input"):
        border1 = coarse_border.shape[2]
        coarse_in, for_a, for_b = call(
            pool_kernel, "coarse_input",
            [rows_of(coarse_total), rows_of(border1), rows_of(border1)],
            [whole_smem] * 2 + [whole_vmem] * 5,
            [pltpu.VMEM((coarse_total, LANES), f32), pltpu.VMEM((2 * border1, LANES), f32)],
            (
                place, coarse_border, local_sums, from_a, from_b,
                pool_target.reshape(2, 1, slots), pool_weight.reshape(2, 1, slots),
            ),
        )
        from_a, from_b = swap_with_neighbours(for_a, for_b)

    with jax.named_scope("coarse_step"):
        edge_total1 = coarse_sender.shape[0]
        block1 = LANES * edge_total1 // coarse_total
        blocks1 = edge_total1 // block1
        share = coarse_total // 8
        coarse_new, own, for_a, for_b = call(
            at_level(coarse_kernel, 1, 9), "coarse_step",
            [rows_of(coarse_total)] + [rows_of(share, f32, 2 * LANES)] * 3,
            [whole_smem, whole_smem] + [whole_vmem] * 7 + weight_specs,
            [
                pltpu.VMEM((coarse_total + 2 * border1, LANES), f32),
                pltpu.VMEM((coarse_total, LANES), bf16),
                pltpu.VMEM((edge_total1, LANES), f32),
                pltpu.VMEM((coarse_total, LANES), bf16),
                pltpu.VMEM((3 * share, 2 * LANES), f32),
            ]
            + weight_scratch,
            (
                place, coarse_sender, coarse_edges, coarse_in, from_a, from_b,
                coarse_receiver.reshape(blocks1, 1, block1), coarse_parent[None, :], coarse_weight[None, :],
            )
            + weights,
        )
        from_a, from_b = swap_with_neighbours(for_a, for_b)
        shares = own + from_a + from_b
        top_in = (shares[:, :LANES] / shares[:, LANES:]).astype(bf16)

    with jax.named_scope("top_step"):
        everyone = gather_all(top_in).reshape(count * share, LANES)
        tile = 2 * share
        window = 3 * tile
        fine_out, coarse_out = call(
            at_level(top_kernel, 2, 9), "top_step",
            [rows_of(fine_total), rows_of(coarse_total)],
            [whole_smem] * 2 + [left_in_hbm] + [whole_vmem] * 6 + weight_specs,
            [
                pltpu.VMEM((fine_total, coarse_total), bf16),
                pltpu.VMEM((count * share, LANES), f32),
                pltpu.VMEM((count * share, LANES), bf16),
                pltpu.VMEM((window, LANES), f32),
                pltpu.SemaphoreType.DMA((fine_total // coarse_total,)),
            ]
            + weight_scratch,
            (
                place, top_sender, lift_picks, top_edges, everyone,
                top_receiver.reshape(top_receiver.shape[0] // tile, 1, tile), coarse_parent[None, :], coarse_new,
                fine_new,
            )
            + weights,
        )
    return (fine_out, coarse_out)


def solution(mesh):
    row = ("groups", "dom")
    return jax.shard_map(
        body,
        mesh=mesh,
        in_specs=(
            P(row, None), P(row, None), P(row), P(row), P(row), P(row, None, None), P(row, None, None),
            P(row, None, None), P(row, None, None), P(row), P(row), P(row, None), P(row), P(row),
            P(row, None, None), P(row), P(row), P("groups", None), P("groups"), P("groups"), P(), P(), P(), P(),
            P(),
        ),
        out_specs=(P(row, None), P(row, None)),
        check_vma=False,
    )
```

```python
import functools

import jax
import jax.numpy as jnp
from jax import lax
from jax.experimental import pallas as pl
from jax.experimental.pallas import tpu as pltpu
from jax.sharding import PartitionSpec as P

epsilon = 1e-05
bf16 = jnp.bfloat16
f32 = jnp.float32
LANES = 128
GROUP = 4
SPLIT = (64, 192, 256, 384)
VMEM_LIMIT = 20 * 2**20
whole_vmem, whole_smem, left_in_hbm = "vmem", "smem", "any"


def mm(a, b):
    return jnp.dot(a, b, preferred_element_type=f32)


def mm_first(a, b):
    return lax.dot_general(a, b, (((0,), (0,)), ((), ())), preferred_element_type=f32)


def gather_rows(index, table_ref, into_ref, count, into_first=0):
    for j in range(count):
        into_ref[pl.ds(into_first + j, 1), :] = table_ref[pl.ds(index(j), 1), :]


def match_rows(ids_row, count, weight_row=None):
    shape = (count, ids_row.shape[1])
    hit = lax.broadcasted_iota(jnp.int32, shape, 0) == ids_row
    if weight_row is None:
        return hit.astype(f32).astype(bf16)
    return jnp.where(hit, weight_row.astype(f32), 0.0).astype(bf16)


def aligned(at, size):
    return pl.ds(pl.multiple_of(at, size), size)


def side_by_side(rows):
    half = rows.shape[0] // 2
    return jnp.concatenate([rows[:half], rows[half:]], axis=1)


def normed_pairs(pairs, w_centred, spread_of):
    centred = mm(pairs, w_centred)
    spread = mm((centred * centred).astype(bf16), spread_of)
    return centred * lax.rsqrt(spread + epsilon)


def with_ones(rows):
    return jnp.concatenate([rows, jnp.ones(rows.shape, bf16)], axis=1)


def fill_weights(edge_out, node_out, w_out, w_node_out, spread_of):
    for weights, into in ((edge_out, w_out), (node_out, w_node_out)):
        wide = weights[...].astype(f32)
        centred = (wide - jnp.mean(wide, axis=1, keepdims=True)).astype(bf16)
        into[...] = jnp.zeros_like(into)
        into[:LANES, :LANES] = centred
        into[LANES:, LANES:] = centred
    shape = spread_of.shape
    same = (lax.broadcasted_iota(jnp.int32, shape, 0) < LANES) == (lax.broadcasted_iota(jnp.int32, shape, 1) < LANES)
    spread_of[...] = jnp.where(same, 1.0 / LANES, 0.0).astype(bf16)


weight_scratch = [pltpu.VMEM((2 * LANES, 2 * LANES), bf16)] * 4


weight_specs = ["level"] * 5


def edge_first(picks, receiver_part, edge_rows, sender_part, w_edge):
    before = mm_first(picks, receiver_part) + mm(edge_rows, w_edge)
    return side_by_side(jnp.maximum(before + sender_part, 0.0).astype(bf16))


def edge_sums(picks, message, gain):
    half = picks.shape[1] // 2
    summed = mm(picks[:, :half], message[:, :LANES]) + mm(picks[:, half:], message[:, LANES:])
    return (summed * gain).astype(bf16)


def node_first(node_rows, summed, w_node):
    hidden = mm(jnp.concatenate([node_rows, summed], axis=1), w_node)
    return side_by_side(jnp.maximum(hidden, 0.0).astype(bf16))


def node_last(node_rows, update, gain):
    update = jnp.concatenate([update[:, :LANES], update[:, LANES:]], axis=0)
    return (node_rows.astype(f32) + update * gain).astype(bf16)


def border_kernel(place_ref, index_ref, x_ref, a_ref, b_ref, table, buffer):
    table[...] = x_ref[...].astype(f32)
    count = a_ref.shape[0]
    for side in range(2):
        gather_rows(lambda j: index_ref[0, side, j], table, buffer, count, side * count)
    a_ref[...] = buffer[aligned(count * place_ref[0], count), :].astype(bf16)
    b_ref[...] = buffer[aligned(count * (1 - place_ref[0]), count), :].astype(bf16)


def fill_table(x_ref, place_ref, from_a, from_b, edge_in, table, receiver_part, w_pairs):
    w_s = edge_in[:LANES, :]
    w_pairs[...] = jnp.zeros_like(w_pairs)
    w_pairs[:LANES, :LANES] = w_s
    w_pairs[LANES:, LANES:] = w_s

    count, border = x_ref.shape[0], from_a.shape[0]
    half = border // 2
    both = mm(x_ref[...], jnp.concatenate([w_s, edge_in[LANES : 2 * LANES, :]], axis=1))
    table[:count, :] = both[:, :LANES]
    receiver_part[...] = both[:, LANES:].astype(bf16)
    for rows, first, scale in (
        (from_a, count + place_ref[0] * border, None),
        (from_b, count + (1 - place_ref[0]) * border, place_ref[1].astype(f32)),
    ):
        both = mm(side_by_side(rows[...]), w_pairs[...])
        if scale is not None:
            both = both * scale
        table[aligned(first, half), :] = both[:, :LANES]
        table[aligned(first + half, half), :] = both[:, LANES:]


def fine_kernel(
    place_ref, pool_index, sender_ref, edge_ref, x_ref, from_a, from_b, receiver_ref, parent_ref,
    weight_ref, edge_in, edge_out, node_in, node_out, gain_ref,
    new_ref, sums_ref, a_ref, b_ref,
    table, receiver_part, new32, buffer, aggregate, node_hidden,
    gathered0, gathered1, hidden0, hidden1, message0, message1,
    index0, index1, index2, index3, index_sem, w_out, w_node_out, spread_of, w_pairs,
):
    gathered, hidden, message = (gathered0, gathered1), (hidden0, hidden1), (message0, message1)
    indices = (index0, index1, index2, index3)
    block = gathered0.shape[0]
    groups, _, group_nodes = parent_ref.shape
    nodes = group_nodes // GROUP
    blocks = groups * GROUP
    gain, node_gain = gain_ref[0:1, :], gain_ref[1:2, :]

    def index_copy(t, k):
        at = aligned(jnp.minimum(t, blocks - 1) * block, block)
        return pltpu.make_async_copy(sender_ref.at[at], indices[k], index_sem.at[k])

    def gather_block(k, into):
        gather_rows(lambda j: indices[k][j], table, into, block)

    for k in range(GROUP):
        index_copy(k, k).start()
    fill_weights(edge_out, node_out, w_out, w_node_out, spread_of)
    fill_table(x_ref, place_ref, from_a, from_b, edge_in, table, receiver_part, w_pairs)
    sums_ref[...] = jnp.zeros_like(sums_ref)
    index_copy(0, 0).wait()
    gather_block(0, gathered0)

    def picks_of(t):
        t = jnp.maximum(t, 0)
        slot = lax.broadcasted_iota(jnp.int32, (1, block), 1) + t * block
        return match_rows(jnp.where(slot < place_ref[2], receiver_ref[t] - t * nodes, -1), nodes)

    def group_step(g, last):
        for k in range(GROUP):
            t = g * GROUP + k
            here, before = k % 2, (k + 1) % 2
            if not last:
                later = (k + 1) % GROUP
                index_copy(t + 1, later).wait()
                index_copy(t + GROUP, k).start()
            keep = {}
            done = jnp.maximum(g - 1, 0)
            rows = aligned(done * group_nodes, group_nodes)

            def pick():
                if not last:
                    keep["picks"] = picks_of(t)
                if not last or k < 2:
                    keep["earlier"] = picks_of(t - 2)

            def multiply_first():
                if not last:
                    keep["before"] = mm_first(
                        keep["picks"], receiver_part[aligned(t * nodes, nodes), :]
                    ) + mm(edge_ref[aligned(t * block, block), :], edge_in[2 * LANES :, :])
                if not last or k < 1:
                    keep["centred"] = mm(hidden[before][...], w_out[...])
                if k == 2:
                    node_hidden[...] = node_first(x_ref[rows, :], aggregate[...], node_in[...])
                if k == 3:
                    keep["node_centred"] = mm(node_hidden[...], w_node_out[...])

            def rectify():
                if not last:
                    rows = jnp.maximum(keep["before"] + gathered[here][...], 0.0)
                    hidden[here][...] = side_by_side(rows.astype(bf16))
                if not last or k < 1:
                    keep["squares"] = (keep["centred"] * keep["centred"]).astype(bf16)
                if k == 3:
                    keep["node_squares"] = (keep["node_centred"] * keep["node_centred"]).astype(bf16)

            def multiply_last():
                if not last or k < 1:
                    keep["spread"] = mm(keep["squares"], spread_of[...])
                if not last or k < 2:
                    into = (k - 2) % GROUP * nodes
                    aggregate[into : into + nodes, :] = edge_sums(keep["earlier"], message[here][...], gain)
                if k == 3:
                    keep["node_spread"] = mm(keep["node_squares"], spread_of[...])

            def scale():
                if not last or k < 1:
                    message[before][...] = (keep["centred"] * lax.rsqrt(keep["spread"] + epsilon)).astype(bf16)
                if k == 3:
                    update = keep["node_centred"] * lax.rsqrt(keep["node_spread"] + epsilon)
                    new_rows = node_last(x_ref[rows, :], update, node_gain)
                    new_ref[rows, :] = new_rows
                    new32[rows, :] = new_rows.astype(f32)
                    shares = match_rows(parent_ref[done], sums_ref.shape[0], weight_ref[done])
                    sums = sums_ref[...] + mm(shares, with_ones(new_rows))
                    sums_ref[...] = sums if last else jnp.where(g > 0, sums, 0.0)

            cuts = (0, *SPLIT, block)
            for i, step in enumerate((pick, multiply_first, rectify, multiply_last, scale)):
                step()
                if not last:
                    gather_rows(
                        lambda j: indices[later][cuts[i] + j], table, gathered[before],
                        cuts[i + 1] - cuts[i], cuts[i],
                    )
    def loop_step(g, carry):
        group_step(g, False)
        return carry

    lax.fori_loop(0, groups, loop_step, 0)
    group_step(groups, True)
    for k in range(1, GROUP):
        index_copy(blocks + k, k).wait()
    count = a_ref.shape[0]
    for side in range(2):
        gather_rows(lambda j: pool_index[0, side, j], new32, buffer, count, side * count)
    a_ref[...] = buffer[aligned(count * place_ref[0], count), :].astype(bf16)
    b_ref[...] = buffer[aligned(count * (1 - place_ref[0]), count), :].astype(bf16)


def pool_kernel(
    place_ref, border_index, sums_ref, from_a, from_b, target_ref, weight_ref,
    coarse_ref, a_ref, b_ref, table, buffer,
):
    count = sums_ref.shape[0]
    total = sums_ref[...]
    for side, rows in ((place_ref[0], from_a), (1 - place_ref[0], from_b)):
        shares = match_rows(target_ref[side], count, weight_ref[side])
        total += mm(shares, with_ones(rows[...]))
    coarse = (total[:, :LANES] / total[:, LANES:]).astype(bf16)
    coarse_ref[...] = coarse
    table[...] = coarse.astype(f32)
    border = a_ref.shape[0]
    for side in range(2):
        gather_rows(lambda j: border_index[0, side, j], table, buffer, border, side * border)
    a_ref[...] = buffer[aligned(border * place_ref[0], border), :].astype(bf16)
    b_ref[...] = buffer[aligned(border * (1 - place_ref[0]), border), :].astype(bf16)


def coarse_kernel(
    place_ref, sender_ref, edge_ref, x_ref, from_a, from_b, receiver_ref, parent_ref, weight_ref,
    edge_in, edge_out, node_in, node_out, gain_ref,
    new_ref, own_ref, a_ref, b_ref,
    table, receiver_part, gathered, aggregate, shares_sum, w_out, w_node_out, spread_of, w_pairs,
):
    blocks, _, block = receiver_ref.shape
    nodes = x_ref.shape[0] // blocks
    fill_weights(edge_out, node_out, w_out, w_node_out, spread_of)
    fill_table(x_ref, place_ref, from_a, from_b, edge_in, table, receiver_part, w_pairs)
    gather_rows(lambda j: sender_ref[j], table, gathered, blocks * block)
    for t in range(blocks):
        at = slice(t * block, (t + 1) * block)
        own = slice(t * nodes, (t + 1) * nodes)
        picks = match_rows(receiver_ref[t] - t * nodes, nodes)
        pairs = edge_first(
            picks, receiver_part[own, :], edge_ref[at, :], gathered[at, :], edge_in[2 * LANES :, :]
        )
        message = normed_pairs(pairs, w_out[...], spread_of[...]).astype(bf16)
        aggregate[own, :] = edge_sums(picks, message, gain_ref[0:1, :])
    pairs = node_first(x_ref[...], aggregate[...], node_in[...])
    new_rows = node_last(x_ref[...], normed_pairs(pairs, w_node_out[...], spread_of[...]), gain_ref[1:2, :])
    new_ref[...] = new_rows
    share = own_ref.shape[0]
    shares = match_rows(parent_ref[...] - (place_ref[3] - 1) * share, 3 * share, weight_ref[...])
    shares_sum[...] = mm(shares, with_ones(new_rows))
    own_ref[...] = shares_sum[share : 2 * share, :]
    a_ref[...] = shares_sum[aligned(2 * share * place_ref[0], share), :]
    b_ref[...] = shares_sum[aligned(2 * share * (1 - place_ref[0]), share), :]


def lift_kernel(parent_ref, picks_ref):
    groups, _, size = parent_ref.shape
    for g in range(groups):
        picks_ref[g * size : (g + 1) * size, :] = match_rows(parent_ref[g], picks_ref.shape[1]).T


def top_kernel(
    place_ref, sender_ref, picks_ref, edge_ref, gathered_in, receiver_ref, parent_ref, coarse_ref,
    fine_ref, edge_in, edge_out, node_in, node_out, gain_ref,
    fine_out, coarse_out,
    table, top_rows, gathered, w_out, w_node_out, spread_of, w_pairs,
):
    chunk = coarse_ref.shape[0]
    chunks = fine_ref.shape[0] // chunk
    tile = receiver_ref.shape[2]
    share = tile // 2
    nodes = 3 * share
    block = 3 * tile
    parts = gathered_in.shape[0] // share
    me, first = place_ref[3], place_ref[4]
    fill_weights(edge_out, node_out, w_out, w_node_out, spread_of)
    sender_part = mm(gathered_in[...], edge_in[:LANES, :])
    for q in range(parts):
        at = aligned((q ^ me) * share, share)
        table[at, :] = sender_part[q * share : (q + 1) * share, :]
        top_rows[at, :] = gathered_in[q * share : (q + 1) * share, :]
    window = top_rows[pl.ds(pl.multiple_of(first * share, share), nodes), :]
    gather_rows(lambda j: sender_ref[first * tile + j], table, gathered, block)
    ids = jnp.concatenate([receiver_ref[first + i] for i in range(3)], axis=1) - first * share
    matches = match_rows(ids, nodes)
    pairs = edge_first(
        matches, mm(window, edge_in[LANES : 2 * LANES, :]).astype(bf16),
        edge_ref[pl.ds(pl.multiple_of(first * tile, tile), block), :], gathered[...], edge_in[2 * LANES :, :],
    )
    message = normed_pairs(pairs, w_out[...], spread_of[...]).astype(bf16)
    pairs = node_first(window, edge_sums(matches, message, gain_ref[0:1, :]), node_in[...])
    top_new = node_last(window, normed_pairs(pairs, w_node_out[...], spread_of[...]), gain_ref[1:2, :])
    up = mm_first(match_rows(parent_ref[...] - first * share, nodes), top_new)
    coarse = (coarse_ref[...].astype(f32) + up).astype(bf16)
    coarse_out[...] = coarse
    for i in range(chunks):
        at = slice(i * chunk, (i + 1) * chunk)
        fine_out[at, :] = (fine_ref[at, :].astype(f32) + mm(picks_ref[at, :], coarse)).astype(bf16)


def call(kernel, name, outs, kinds, scratch, operands, level=None, us=1.0):
    def with_level(*refs):
        kernel(*[
            ref.at[level] if i < len(kinds) and kinds[i] == "level" else ref for i, ref in enumerate(refs)
        ])

    spaces = {whole_smem: pltpu.SMEM, left_in_hbm: pl.ANY}
    return pl.pallas_call(
        with_level,
        name=name,
        out_shape=outs,
        in_specs=[pl.BlockSpec(memory_space=spaces.get(kind, pltpu.VMEM)) for kind in kinds],
        out_specs=jax.tree.map(lambda _: pl.BlockSpec(memory_space=pltpu.VMEM), outs),
        scratch_shapes=scratch,
        cost_estimate=pl.CostEstimate(flops=int(us * 10**9), bytes_accessed=0, transcendentals=0),
        compiler_params=pltpu.CompilerParams(vmem_limit_bytes=VMEM_LIMIT),
    )(*operands)


def rows_of(count, dtype=bf16, width=LANES):
    return jax.ShapeDtypeStruct((count, width), dtype)


def swap_with_neighbours(for_a, for_b):
    count = lax.axis_size("dom")
    pairs_a = [(i, i ^ 1) for i in range(count)]
    pairs_b = [(i, (i + 1) % count) for i in range(1, count, 2)]
    pairs_b += [(j, i) for i, j in pairs_b]
    return lax.ppermute(for_a, "dom", pairs_a), lax.ppermute(for_b, "dom", pairs_b)


def gather_all(rows):
    count = lax.axis_size("dom")
    steps = []
    stride = 1
    while stride < count:
        radix = 4 if stride * 4 <= count else 2
        steps.append((stride, radix))
        stride *= radix
    blocks = rows[None]
    for stride, radix in reversed(steps):
        taken = [blocks] + [
            lax.ppermute(blocks, "dom", [(i, i ^ (j * stride)) for i in range(count)])
            for j in range(1, radix)
        ]
        blocks = jnp.stack(taken, axis=1).reshape((-1,) + rows.shape)
    return blocks


def body(
    fine_latent, fine_edges, fine_sender, fine_receiver, edge_count, fine_border, pool_rows, pool_target,
    pool_weight, fine_parent, fine_weight, coarse_edges, coarse_sender, coarse_receiver, coarse_border,
    coarse_parent, coarse_weight, top_edges, top_sender, top_receiver, edge_in, edge_out, node_in, node_out,
    norm_gain,
):
    count = lax.axis_size("dom")
    me = lax.axis_index("dom").astype(jnp.int32)
    inner = jnp.where((me == 0) | (me == count - 1), 0, 1).astype(jnp.int32)
    place = jnp.stack([1 - me % 2, inner, edge_count[0], me, jnp.clip(me - 1, 0, count - 3)])
    weights = (edge_in, edge_out, node_in, node_out, norm_gain)

    fine_total = fine_latent.shape[0]
    edge_total = fine_sender.shape[0]
    coarse_total = coarse_parent.shape[0]
    border = fine_border.shape[2]
    slots = pool_rows.shape[2]
    nodes = LANES
    block = nodes * edge_total // fine_total
    blocks = edge_total // block
    groups = blocks // GROUP

    with jax.named_scope("fine_border_rows"):
        for_a, for_b = call(
            border_kernel, "border_rows", [rows_of(border), rows_of(border)],
            [whole_smem, whole_smem, whole_vmem],
            [pltpu.VMEM((fine_total, LANES), f32), pltpu.VMEM((2 * border, LANES), f32)],
            (place, fine_border, fine_latent),
            us=3.0,
        )
        from_a, from_b = swap_with_neighbours(for_a, for_b)
        lift_picks = call(
            lift_kernel, "lift_picks", rows_of(fine_total, bf16, coarse_total), [whole_vmem], [],
            (fine_parent.reshape(fine_total // coarse_total, 1, coarse_total),),
            us=3.0,
        )

    with jax.named_scope("fine_step"):
        fine_new, local_sums, for_a, for_b = call(
            fine_kernel, "fine_step",
            [rows_of(fine_total), rows_of(coarse_total, f32, 2 * LANES), rows_of(slots), rows_of(slots)],
            [whole_smem, whole_smem, left_in_hbm] + [whole_vmem] * 7 + weight_specs,
            [
                pltpu.VMEM((fine_total + 2 * border, LANES), f32),
                pltpu.VMEM((fine_total, LANES), bf16),
                pltpu.VMEM((fine_total, LANES), f32),
                pltpu.VMEM((2 * slots, LANES), f32),
                pltpu.VMEM((GROUP * nodes, LANES), bf16),
                pltpu.VMEM((GROUP * nodes // 2, 2 * LANES), bf16),
            ]
            + [pltpu.VMEM((block, LANES), f32)] * 2
            + [pltpu.VMEM((block // 2, 2 * LANES), bf16)] * 4
            + [pltpu.SMEM((block,), jnp.int32)] * GROUP
            + [pltpu.SemaphoreType.DMA((GROUP,))]
            + weight_scratch,
            (
                place, pool_rows, fine_sender, fine_edges, fine_latent, from_a, from_b,
                fine_receiver.reshape(blocks, 1, block), fine_parent.reshape(groups, 1, GROUP * nodes),
                fine_weight.reshape(groups, 1, GROUP * nodes),
            )
            + weights,
            level=0,
            us=24.0,
        )
        from_a, from_b = swap_with_neighbours(for_a, for_b)

    with jax.named_scope("coarse_input"):
        border1 = coarse_border.shape[2]
        coarse_in, for_a, for_b = call(
            pool_kernel, "coarse_input",
            [rows_of(coarse_total), rows_of(border1), rows_of(border1)],
            [whole_smem, whole_smem] + [whole_vmem] * 5,
            [pltpu.VMEM((coarse_total, LANES), f32), pltpu.VMEM((2 * border1, LANES), f32)],
            (
                place, coarse_border, local_sums, from_a, from_b,
                pool_target.reshape(2, 1, slots), pool_weight.reshape(2, 1, slots),
            ),
        )
        from_a, from_b = swap_with_neighbours(for_a, for_b)

    with jax.named_scope("coarse_step"):
        edge_total1 = coarse_sender.shape[0]
        block1 = LANES * edge_total1 // coarse_total
        blocks1 = edge_total1 // block1
        share = coarse_total // 8
        coarse_new, own, for_a, for_b = call(
            coarse_kernel, "coarse_step",
            [rows_of(coarse_total)] + [rows_of(share, f32, 2 * LANES)] * 3,
            [whole_smem, whole_smem] + [whole_vmem] * 7 + weight_specs,
            [
                pltpu.VMEM((coarse_total + 2 * border1, LANES), f32),
                pltpu.VMEM((coarse_total, LANES), bf16),
                pltpu.VMEM((edge_total1, LANES), f32),
                pltpu.VMEM((coarse_total, LANES), bf16),
                pltpu.VMEM((3 * share, 2 * LANES), f32),
            ]
            + weight_scratch,
            (
                place, coarse_sender, coarse_edges, coarse_in, from_a, from_b,
                coarse_receiver.reshape(blocks1, 1, block1), coarse_parent[None, :], coarse_weight[None, :],
            )
            + weights,
            level=1,
            us=4.0,
        )
        from_a, from_b = swap_with_neighbours(for_a, for_b)
        shares = own + from_a + from_b
        top_in = (shares[:, :LANES] / shares[:, LANES:]).astype(bf16)

    with jax.named_scope("top_step"):
        everyone = gather_all(top_in).reshape(count * share, LANES)
        tile = 2 * share
        window = 3 * tile
        fine_out, coarse_out = call(
            top_kernel, "top_step",
            [rows_of(fine_total), rows_of(coarse_total)],
            [whole_smem, whole_smem] + [whole_vmem] * 7 + weight_specs,
            [
                pltpu.VMEM((count * share, LANES), f32),
                pltpu.VMEM((count * share, LANES), bf16),
                pltpu.VMEM((window, LANES), f32),
            ]
            + weight_scratch,
            (
                place, top_sender, lift_picks, top_edges, everyone,
                top_receiver.reshape(top_receiver.shape[0] // tile, 1, tile), coarse_parent[None, :], coarse_new,
                fine_new,
            )
            + weights,
            level=2,
            us=5.0,
        )
    return (fine_out, coarse_out)


def solution(mesh):
    row = ("groups", "dom")
    return jax.shard_map(
        body,
        mesh=mesh,
        in_specs=(
            P(row, None), P(row, None), P(row), P(row), P(row), P(row, None, None), P(row, None, None),
            P(row, None, None), P(row, None, None), P(row), P(row), P(row, None), P(row), P(row),
            P(row, None, None), P(row), P(row), P("groups", None), P("groups"), P("groups"), P(), P(), P(), P(),
            P(),
        ),
        out_specs=(P(row, None), P(row, None)),
        check_vma=False,
    )
```

```python
import functools

import jax
import jax.numpy as jnp
from jax import lax
from jax.experimental import pallas as pl
from jax.experimental.pallas import tpu as pltpu
from jax.sharding import PartitionSpec as P

epsilon = 1e-05
bf16 = jnp.bfloat16
f32 = jnp.float32
LANES = 128
GROUP = 4
SPLIT = (64, 192, 256, 384)
VMEM_LIMIT = 20 * 2**20
whole_vmem, whole_smem, left_in_hbm = "vmem", "smem", "any"


def mm(a, b):
    return jnp.dot(a, b, preferred_element_type=f32)


def mm_first(a, b):
    return lax.dot_general(a, b, (((0,), (0,)), ((), ())), preferred_element_type=f32)


def gather_rows(index, table_ref, into_ref, count, into_first=0):
    for j in range(count):
        into_ref[pl.ds(into_first + j, 1), :] = table_ref[pl.ds(index(j), 1), :]


def match_rows(ids_row, count, weight_row=None):
    shape = (count, ids_row.shape[1])
    hit = lax.broadcasted_iota(jnp.int32, shape, 0) == ids_row
    if weight_row is None:
        return hit.astype(f32).astype(bf16)
    return jnp.where(hit, weight_row.astype(f32), 0.0).astype(bf16)


def aligned(at, size):
    return pl.ds(pl.multiple_of(at, size), size)


def side_by_side(rows):
    half = rows.shape[0] // 2
    return jnp.concatenate([rows[:half], rows[half:]], axis=1)


def normed_pairs(pairs, w_centred, spread_of):
    centred = mm(pairs, w_centred)
    spread = mm((centred * centred).astype(bf16), spread_of)
    return centred * lax.rsqrt(spread + epsilon)


def with_ones(rows):
    return jnp.concatenate([rows, jnp.ones(rows.shape, bf16)], axis=1)


def fill_weights(edge_out, node_out, w_out, w_node_out, spread_of):
    for weights, into in ((edge_out, w_out), (node_out, w_node_out)):
        wide = weights[...].astype(f32)
        centred = (wide - jnp.mean(wide, axis=1, keepdims=True)).astype(bf16)
        into[...] = jnp.zeros_like(into)
        into[:LANES, :LANES] = centred
        into[LANES:, LANES:] = centred
    shape = spread_of.shape
    same = (lax.broadcasted_iota(jnp.int32, shape, 0) < LANES) == (lax.broadcasted_iota(jnp.int32, shape, 1) < LANES)
    spread_of[...] = jnp.where(same, 1.0 / LANES, 0.0).astype(bf16)


weight_scratch = [pltpu.VMEM((2 * LANES, 2 * LANES), bf16)] * 4


weight_specs = ["level"] * 5


def edge_first(picks, receiver_part, edge_rows, sender_part, w_edge):
    before = mm_first(picks, receiver_part) + mm(edge_rows, w_edge)
    return side_by_side(jnp.maximum(before + sender_part, 0.0).astype(bf16))


def edge_sums(picks, message, gain):
    half = picks.shape[1] // 2
    summed = mm(picks[:, :half], message[:, :LANES]) + mm(picks[:, half:], message[:, LANES:])
    return (summed * gain).astype(bf16)


def node_first(node_rows, summed, w_node):
    hidden = mm(jnp.concatenate([node_rows, summed], axis=1), w_node)
    return side_by_side(jnp.maximum(hidden, 0.0).astype(bf16))


def node_last(node_rows, update, gain):
    update = jnp.concatenate([update[:, :LANES], update[:, LANES:]], axis=0)
    return (node_rows.astype(f32) + update * gain).astype(bf16)


def border_kernel(place_ref, index_ref, x_ref, a_ref, b_ref, table, buffer):
    table[...] = x_ref[...].astype(f32)
    count = a_ref.shape[0]
    for side in range(2):
        gather_rows(lambda j: index_ref[0, side, j], table, buffer, count, side * count)
    a_ref[...] = buffer[aligned(count * place_ref[0], count), :].astype(bf16)
    b_ref[...] = buffer[aligned(count * (1 - place_ref[0]), count), :].astype(bf16)


def fill_table(x_ref, place_ref, from_a, from_b, edge_in, table, receiver_part, w_pairs):
    w_s = edge_in[:LANES, :]
    w_pairs[...] = jnp.zeros_like(w_pairs)
    w_pairs[:LANES, :LANES] = w_s
    w_pairs[LANES:, LANES:] = w_s

    count, border = x_ref.shape[0], from_a.shape[0]
    half = border // 2
    both = mm(x_ref[...], jnp.concatenate([w_s, edge_in[LANES : 2 * LANES, :]], axis=1))
    table[:count, :] = both[:, :LANES]
    receiver_part[...] = both[:, LANES:].astype(bf16)
    for rows, first, scale in (
        (from_a, count + place_ref[0] * border, None),
        (from_b, count + (1 - place_ref[0]) * border, place_ref[1].astype(f32)),
    ):
        both = mm(side_by_side(rows[...]), w_pairs[...])
        if scale is not None:
            both = both * scale
        table[aligned(first, half), :] = both[:, :LANES]
        table[aligned(first + half, half), :] = both[:, LANES:]


def fine_kernel(
    place_ref, pool_index, sender_ref, edge_ref, x_ref, from_a, from_b, receiver_ref,
    edge_in, edge_out, node_in, node_out, gain_ref,
    new_ref, a_ref, b_ref,
    table, receiver_part, new32, buffer, aggregate, node_hidden,
    gathered0, gathered1, hidden0, hidden1, message0, message1,
    index0, index1, index2, index3, index_sem, w_out, w_node_out, spread_of, w_pairs,
):
    gathered, hidden, message = (gathered0, gathered1), (hidden0, hidden1), (message0, message1)
    indices = (index0, index1, index2, index3)
    block = gathered0.shape[0]
    blocks = receiver_ref.shape[0]
    groups = blocks // GROUP
    nodes = x_ref.shape[0] // blocks
    group_nodes = GROUP * nodes
    gain, node_gain = gain_ref[0:1, :], gain_ref[1:2, :]

    def index_copy(t, k):
        at = aligned(jnp.minimum(t, blocks - 1) * block, block)
        return pltpu.make_async_copy(sender_ref.at[at], indices[k], index_sem.at[k])

    def gather_block(k, into):
        gather_rows(lambda j: indices[k][j], table, into, block)

    for k in range(GROUP):
        index_copy(k, k).start()
    fill_weights(edge_out, node_out, w_out, w_node_out, spread_of)
    fill_table(x_ref, place_ref, from_a, from_b, edge_in, table, receiver_part, w_pairs)
    index_copy(0, 0).wait()
    gather_block(0, gathered0)

    def picks_of(t):
        t = jnp.maximum(t, 0)
        slot = lax.broadcasted_iota(jnp.int32, (1, block), 1) + t * block
        return match_rows(jnp.where(slot < place_ref[2], receiver_ref[t] - t * nodes, -1), nodes)

    def group_step(g, last):
        for k in range(GROUP):
            t = g * GROUP + k
            here, before = k % 2, (k + 1) % 2
            if not last:
                later = (k + 1) % GROUP
                index_copy(t + 1, later).wait()
                index_copy(t + GROUP, k).start()
            keep = {}
            done = jnp.maximum(g - 1, 0)
            rows = aligned(done * group_nodes, group_nodes)

            def pick():
                if not last:
                    keep["picks"] = picks_of(t)
                if not last or k < 2:
                    keep["earlier"] = picks_of(t - 2)

            def multiply_first():
                if not last:
                    keep["before"] = mm_first(
                        keep["picks"], receiver_part[aligned(t * nodes, nodes), :]
                    ) + mm(edge_ref[aligned(t * block, block), :], edge_in[2 * LANES :, :])
                if not last or k < 1:
                    keep["centred"] = mm(hidden[before][...], w_out[...])
                if k == 2:
                    node_hidden[...] = node_first(x_ref[rows, :], aggregate[...], node_in[...])
                if k == 3:
                    keep["node_centred"] = mm(node_hidden[...], w_node_out[...])

            def rectify():
                if not last:
                    rows = jnp.maximum(keep["before"] + gathered[here][...], 0.0)
                    hidden[here][...] = side_by_side(rows.astype(bf16))
                if not last or k < 1:
                    keep["squares"] = (keep["centred"] * keep["centred"]).astype(bf16)
                if k == 3:
                    keep["node_squares"] = (keep["node_centred"] * keep["node_centred"]).astype(bf16)

            def multiply_last():
                if not last or k < 1:
                    keep["spread"] = mm(keep["squares"], spread_of[...])
                if not last or k < 2:
                    into = (k - 2) % GROUP * nodes
                    aggregate[into : into + nodes, :] = edge_sums(keep["earlier"], message[here][...], gain)
                if k == 3:
                    keep["node_spread"] = mm(keep["node_squares"], spread_of[...])

            def scale():
                if not last or k < 1:
                    message[before][...] = (keep["centred"] * lax.rsqrt(keep["spread"] + epsilon)).astype(bf16)
                if k == 3:
                    update = keep["node_centred"] * lax.rsqrt(keep["node_spread"] + epsilon)
                    new_rows = node_last(x_ref[rows, :], update, node_gain)
                    new_ref[rows, :] = new_rows
                    new32[rows, :] = new_rows.astype(f32)

            cuts = (0, *SPLIT, block)
            for i, step in enumerate((pick, multiply_first, rectify, multiply_last, scale)):
                step()
                if not last:
                    gather_rows(
                        lambda j: indices[later][cuts[i] + j], table, gathered[before],
                        cuts[i + 1] - cuts[i], cuts[i],
                    )
    def loop_step(g, carry):
        group_step(g, False)
        return carry

    lax.fori_loop(0, groups, loop_step, 0)
    group_step(groups, True)
    for k in range(1, GROUP):
        index_copy(blocks + k, k).wait()
    count = a_ref.shape[0]
    for side in range(2):
        gather_rows(lambda j: pool_index[0, side, j], new32, buffer, count, side * count)
    a_ref[...] = buffer[aligned(count * place_ref[0], count), :].astype(bf16)
    b_ref[...] = buffer[aligned(count * (1 - place_ref[0]), count), :].astype(bf16)


def local_pool_kernel(new_ref, parent_ref, weight_ref, sums_ref):
    groups, _, size = parent_ref.shape
    total = 0.0
    for g in range(groups):
        shares = match_rows(parent_ref[g], sums_ref.shape[0], weight_ref[g])
        total += mm(shares, with_ones(new_ref[g * size : (g + 1) * size, :]))
    sums_ref[...] = total


def pool_kernel(
    place_ref, border_index, sums_ref, from_a, from_b, target_ref, weight_ref,
    coarse_ref, a_ref, b_ref, table, buffer,
):
    count = sums_ref.shape[0]
    total = sums_ref[...]
    for side, rows in ((place_ref[0], from_a), (1 - place_ref[0], from_b)):
        shares = match_rows(target_ref[side], count, weight_ref[side])
        total += mm(shares, with_ones(rows[...]))
    coarse = (total[:, :LANES] / total[:, LANES:]).astype(bf16)
    coarse_ref[...] = coarse
    table[...] = coarse.astype(f32)
    border = a_ref.shape[0]
    for side in range(2):
        gather_rows(lambda j: border_index[0, side, j], table, buffer, border, side * border)
    a_ref[...] = buffer[aligned(border * place_ref[0], border), :].astype(bf16)
    b_ref[...] = buffer[aligned(border * (1 - place_ref[0]), border), :].astype(bf16)


def coarse_kernel(
    place_ref, sender_ref, edge_ref, x_ref, from_a, from_b, receiver_ref, parent_ref, weight_ref,
    edge_in, edge_out, node_in, node_out, gain_ref,
    new_ref, own_ref, a_ref, b_ref,
    table, receiver_part, gathered, aggregate, shares_sum, w_out, w_node_out, spread_of, w_pairs,
):
    blocks, _, block = receiver_ref.shape
    nodes = x_ref.shape[0] // blocks
    fill_weights(edge_out, node_out, w_out, w_node_out, spread_of)
    fill_table(x_ref, place_ref, from_a, from_b, edge_in, table, receiver_part, w_pairs)
    keep = {}

    def gather_part(t, part):
        if t < blocks:
            begin = t * block + part * block // 4
            gather_rows(lambda j: sender_ref[begin + j], table, gathered, block // 4, begin)

    def first(t):
        own, at = slice(t * nodes, (t + 1) * nodes), slice(t * block, (t + 1) * block)
        keep["picks", t] = match_rows(receiver_ref[t] - t * nodes, nodes)
        keep["pairs", t] = edge_first(
            keep["picks", t], receiver_part[own, :], edge_ref[at, :], gathered[at, :], edge_in[2 * LANES :, :]
        )

    def second(t):
        keep["centred", t] = mm(keep["pairs", t], w_out[...])

    def third(t):
        centred = keep["centred", t]
        spread = mm((centred * centred).astype(bf16), spread_of[...])
        keep["message", t] = (centred * lax.rsqrt(spread + epsilon)).astype(bf16)

    def sum_edges(t):
        own = slice(t * nodes, (t + 1) * nodes)
        aggregate[own, :] = edge_sums(keep["picks", t], keep["message", t], gain_ref[0:1, :])

    for part in range(4):
        gather_part(0, part)
    for tick in range(blocks + 3):
        for part, (stage, lag) in enumerate(((first, 0), (second, 1), (third, 2), (sum_edges, 3))):
            if 0 <= tick - lag < blocks:
                stage(tick - lag)
            gather_part(tick + 1, part)
    pairs = node_first(x_ref[...], aggregate[...], node_in[...])
    new_rows = node_last(x_ref[...], normed_pairs(pairs, w_node_out[...], spread_of[...]), gain_ref[1:2, :])
    new_ref[...] = new_rows
    share = x_ref.shape[0] // 8
    size = own_ref.shape[0]
    shares = match_rows(parent_ref[...] - (place_ref[3] - 1) * share, 3 * share, weight_ref[...])
    sums = mm(shares, new_rows)
    rest = jnp.zeros((LANES - share, shares.shape[1]), bf16)
    for i in range(3):
        at = slice(i * share, (i + 1) * share)
        shares_sum[i * size : i * size + share, :] = sums[at]
        shares_sum[i * size + share : (i + 1) * size, :] = lax.dot_general(
            jnp.ones((size - share, shares.shape[1]), bf16), jnp.concatenate([shares[at], rest], axis=0),
            (((1,), (1,)), ((), ())), preferred_element_type=f32,
        )
    own_ref[...] = shares_sum[size : 2 * size, :]
    a_ref[...] = shares_sum[aligned(2 * size * place_ref[0], size), :]
    b_ref[...] = shares_sum[aligned(2 * size * (1 - place_ref[0]), size), :]


def lift_kernel(parent_ref, picks_ref):
    groups, _, size = parent_ref.shape
    for g in range(groups):
        picks_ref[g * size : (g + 1) * size, :] = match_rows(parent_ref[g], picks_ref.shape[1]).T


def top_kernel(
    place_ref, sender_ref, picks_ref, edge_ref, gathered_in, receiver_ref, parent_ref, coarse_ref,
    fine_ref, edge_in, edge_out, node_in, node_out, gain_ref,
    fine_out, coarse_out,
    table, top_rows, gathered, w_out, w_node_out, spread_of, w_pairs,
):
    chunk = coarse_ref.shape[0]
    chunks = fine_ref.shape[0] // chunk
    tile = receiver_ref.shape[2]
    share = tile // 2
    nodes = 3 * share
    block = 3 * tile
    parts = gathered_in.shape[0] // share
    me, first = place_ref[3], place_ref[4]
    fill_weights(edge_out, node_out, w_out, w_node_out, spread_of)
    sender_part = mm(gathered_in[...], edge_in[:LANES, :])
    for q in range(parts):
        at = aligned((q ^ me) * share, share)
        table[at, :] = sender_part[q * share : (q + 1) * share, :]
        top_rows[at, :] = gathered_in[q * share : (q + 1) * share, :]
    window = top_rows[pl.ds(pl.multiple_of(first * share, share), nodes), :]
    gather_rows(lambda j: sender_ref[first * tile + j], table, gathered, block)
    ids = jnp.concatenate([receiver_ref[first + i] for i in range(3)], axis=1) - first * share
    matches = match_rows(ids, nodes)
    pairs = edge_first(
        matches, mm(window, edge_in[LANES : 2 * LANES, :]).astype(bf16),
        edge_ref[pl.ds(pl.multiple_of(first * tile, tile), block), :], gathered[...], edge_in[2 * LANES :, :],
    )
    message = normed_pairs(pairs, w_out[...], spread_of[...]).astype(bf16)
    pairs = node_first(window, edge_sums(matches, message, gain_ref[0:1, :]), node_in[...])
    top_new = node_last(window, normed_pairs(pairs, w_node_out[...], spread_of[...]), gain_ref[1:2, :])
    up = mm_first(match_rows(parent_ref[...] - first * share, nodes), top_new)
    coarse = (coarse_ref[...].astype(f32) + up).astype(bf16)
    coarse_out[...] = coarse
    for i in range(chunks):
        at = slice(i * chunk, (i + 1) * chunk)
        fine_out[at, :] = (fine_ref[at, :].astype(f32) + mm(picks_ref[at, :], coarse)).astype(bf16)


def call(kernel, name, outs, kinds, scratch, operands, level=None, us=1.0):
    def with_level(*refs):
        kernel(*[
            ref.at[level] if i < len(kinds) and kinds[i] == "level" else ref for i, ref in enumerate(refs)
        ])

    spaces = {whole_smem: pltpu.SMEM, left_in_hbm: pl.ANY}
    return pl.pallas_call(
        with_level,
        name=name,
        out_shape=outs,
        in_specs=[pl.BlockSpec(memory_space=spaces.get(kind, pltpu.VMEM)) for kind in kinds],
        out_specs=jax.tree.map(lambda _: pl.BlockSpec(memory_space=pltpu.VMEM), outs),
        scratch_shapes=scratch,
        cost_estimate=pl.CostEstimate(flops=int(us * 10**9), bytes_accessed=0, transcendentals=0),
        compiler_params=pltpu.CompilerParams(vmem_limit_bytes=VMEM_LIMIT),
    )(*operands)


def rows_of(count, dtype=bf16, width=LANES):
    return jax.ShapeDtypeStruct((count, width), dtype)


def swap_with_neighbours(for_a, for_b):
    count = lax.axis_size("dom")
    pairs_a = [(i, i ^ 1) for i in range(count)]
    pairs_b = [(i, (i + 1) % count) for i in range(1, count, 2)]
    pairs_b += [(j, i) for i, j in pairs_b]
    return lax.ppermute(for_a, "dom", pairs_a), lax.ppermute(for_b, "dom", pairs_b)


def gather_all(rows):
    count = lax.axis_size("dom")
    steps = []
    stride = 1
    while stride < count:
        radix = 4 if stride * 4 <= count else 2
        steps.append((stride, radix))
        stride *= radix
    blocks = rows[None]
    for stride, radix in reversed(steps):
        taken = [blocks] + [
            lax.ppermute(blocks, "dom", [(i, i ^ (j * stride)) for i in range(count)])
            for j in range(1, radix)
        ]
        blocks = jnp.stack(taken, axis=1).reshape((-1,) + rows.shape)
    return blocks


def body(
    fine_latent, fine_edges, fine_sender, fine_receiver, edge_count, fine_border, pool_rows, pool_target,
    pool_weight, fine_parent, fine_weight, coarse_edges, coarse_sender, coarse_receiver, coarse_border,
    coarse_parent, coarse_weight, top_edges, top_sender, top_receiver, edge_in, edge_out, node_in, node_out,
    norm_gain,
):
    count = lax.axis_size("dom")
    me = lax.axis_index("dom").astype(jnp.int32)
    inner = jnp.where((me == 0) | (me == count - 1), 0, 1).astype(jnp.int32)
    place = jnp.stack([1 - me % 2, inner, edge_count[0], me, jnp.clip(me - 1, 0, count - 3)])
    weights = (edge_in, edge_out, node_in, node_out, norm_gain)

    fine_total = fine_latent.shape[0]
    edge_total = fine_sender.shape[0]
    coarse_total = coarse_parent.shape[0]
    border = fine_border.shape[2]
    slots = pool_rows.shape[2]
    nodes = LANES
    block = nodes * edge_total // fine_total
    blocks = edge_total // block
    groups = blocks // GROUP

    with jax.named_scope("fine_border_rows"):
        for_a, for_b = call(
            border_kernel, "border_rows", [rows_of(border), rows_of(border)],
            [whole_smem, whole_smem, whole_vmem],
            [pltpu.VMEM((fine_total, LANES), f32), pltpu.VMEM((2 * border, LANES), f32)],
            (place, fine_border, fine_latent),
            us=3.0,
        )
        from_a, from_b = swap_with_neighbours(for_a, for_b)
        lift_picks = call(
            lift_kernel, "lift_picks", rows_of(fine_total, bf16, coarse_total), [whole_vmem], [],
            (fine_parent.reshape(fine_total // coarse_total, 1, coarse_total),),
            us=3.0,
        )

    with jax.named_scope("fine_step"):
        fine_new, for_a, for_b = call(
            fine_kernel, "fine_step",
            [rows_of(fine_total), rows_of(slots), rows_of(slots)],
            [whole_smem, whole_smem, left_in_hbm] + [whole_vmem] * 5 + weight_specs,
            [
                pltpu.VMEM((fine_total + 2 * border, LANES), f32),
                pltpu.VMEM((fine_total, LANES), bf16),
                pltpu.VMEM((fine_total, LANES), f32),
                pltpu.VMEM((2 * slots, LANES), f32),
                pltpu.VMEM((GROUP * nodes, LANES), bf16),
                pltpu.VMEM((GROUP * nodes // 2, 2 * LANES), bf16),
            ]
            + [pltpu.VMEM((block, LANES), f32)] * 2
            + [pltpu.VMEM((block // 2, 2 * LANES), bf16)] * 4
            + [pltpu.SMEM((block,), jnp.int32)] * GROUP
            + [pltpu.SemaphoreType.DMA((GROUP,))]
            + weight_scratch,
            (
                place, pool_rows, fine_sender, fine_edges, fine_latent, from_a, from_b,
                fine_receiver.reshape(blocks, 1, block),
            )
            + weights,
            level=0,
            us=24.0,
        )
        from_a, from_b = swap_with_neighbours(for_a, for_b)
        by_group = (groups, 1, GROUP * nodes)
        local_sums = call(
            local_pool_kernel, "local_pool_step", rows_of(coarse_total, f32, 2 * LANES), [whole_vmem] * 3, [],
            (fine_new, fine_parent.reshape(by_group), fine_weight.reshape(by_group)),
            us=2.0,
        )

    with jax.named_scope("coarse_input"):
        border1 = coarse_border.shape[2]
        coarse_in, for_a, for_b = call(
            pool_kernel, "coarse_input",
            [rows_of(coarse_total), rows_of(border1), rows_of(border1)],
            [whole_smem, whole_smem] + [whole_vmem] * 5,
            [pltpu.VMEM((coarse_total, LANES), f32), pltpu.VMEM((2 * border1, LANES), f32)],
            (
                place, coarse_border, local_sums, from_a, from_b,
                pool_target.reshape(2, 1, slots), pool_weight.reshape(2, 1, slots),
            ),
        )
        from_a, from_b = swap_with_neighbours(for_a, for_b)

    with jax.named_scope("coarse_step"):
        edge_total1 = coarse_sender.shape[0]
        block1 = LANES * edge_total1 // coarse_total
        blocks1 = edge_total1 // block1
        share = coarse_total // 8
        coarse_new, own, for_a, for_b = call(
            coarse_kernel, "coarse_step",
            [rows_of(coarse_total)] + [rows_of(share + 8, f32)] * 3,
            [whole_smem, whole_smem] + [whole_vmem] * 7 + weight_specs,
            [
                pltpu.VMEM((coarse_total + 2 * border1, LANES), f32),
                pltpu.VMEM((coarse_total, LANES), bf16),
                pltpu.VMEM((edge_total1, LANES), f32),
                pltpu.VMEM((coarse_total, LANES), bf16),
                pltpu.VMEM((3 * (share + 8), LANES), f32),
            ]
            + weight_scratch,
            (
                place, coarse_sender, coarse_edges, coarse_in, from_a, from_b,
                coarse_receiver.reshape(blocks1, 1, block1), coarse_parent[None, :], coarse_weight[None, :],
            )
            + weights,
            level=1,
            us=4.0,
        )
        from_a, from_b = swap_with_neighbours(for_a, for_b)
        shares = own + from_a + from_b
        top_in = (shares[:share] / shares[share, :share][:, None]).astype(bf16)

    with jax.named_scope("top_step"):
        everyone = gather_all(top_in).reshape(count * share, LANES)
        tile = 2 * share
        window = 3 * tile
        fine_out, coarse_out = call(
            top_kernel, "top_step",
            [rows_of(fine_total), rows_of(coarse_total)],
            [whole_smem, whole_smem] + [whole_vmem] * 7 + weight_specs,
            [
                pltpu.VMEM((count * share, LANES), f32),
                pltpu.VMEM((count * share, LANES), bf16),
                pltpu.VMEM((window, LANES), f32),
            ]
            + weight_scratch,
            (
                place, top_sender, lift_picks, top_edges, everyone,
                top_receiver.reshape(top_receiver.shape[0] // tile, 1, tile), coarse_parent[None, :], coarse_new,
                fine_new,
            )
            + weights,
            level=2,
            us=5.0,
        )
    return (fine_out, coarse_out)


def solution(mesh):
    row = ("groups", "dom")
    return jax.shard_map(
        body,
        mesh=mesh,
        in_specs=(
            P(row, None), P(row, None), P(row), P(row), P(row), P(row, None, None), P(row, None, None),
            P(row, None, None), P(row, None, None), P(row), P(row), P(row, None), P(row), P(row),
            P(row, None, None), P(row), P(row), P("groups", None), P("groups"), P("groups"), P(), P(), P(), P(),
            P(),
        ),
        out_specs=(P(row, None), P(row, None)),
        check_vma=False,
    )
```

```python
import functools

import jax
import jax.numpy as jnp
from jax import lax
from jax.experimental import pallas as pl
from jax.experimental.pallas import tpu as pltpu
from jax.sharding import PartitionSpec as P

epsilon = 1e-05
bf16 = jnp.bfloat16
f32 = jnp.float32
LANES = 128
GROUP = 4
SPLIT = (64, 192, 256, 384)
VMEM_LIMIT = 20 * 2**20
whole_vmem, whole_smem, left_in_hbm = "vmem", "smem", "any"


def mm(a, b):
    return jnp.dot(a, b, preferred_element_type=f32)


def mm_first(a, b):
    return lax.dot_general(a, b, (((0,), (0,)), ((), ())), preferred_element_type=f32)


def gather_rows(index, table_ref, into_ref, count, into_first=0):
    for j in range(count):
        into_ref[pl.ds(into_first + j, 1), :] = table_ref[pl.ds(index(j), 1), :]


def match_rows(ids_row, count, weight_row=None):
    shape = (count, ids_row.shape[1])
    hit = lax.broadcasted_iota(jnp.int32, shape, 0) == ids_row
    if weight_row is None:
        return hit.astype(f32).astype(bf16)
    return jnp.where(hit, weight_row.astype(f32), 0.0).astype(bf16)


def aligned(at, size):
    return pl.ds(pl.multiple_of(at, size), size)


def side_by_side(rows):
    half = rows.shape[0] // 2
    return jnp.concatenate([rows[:half], rows[half:]], axis=1)


def normed_pairs(pairs, w_centred, spread_of):
    centred = mm(pairs, w_centred)
    spread = mm((centred * centred).astype(bf16), spread_of)
    return centred * lax.rsqrt(spread + epsilon)


def with_ones(rows):
    return jnp.concatenate([rows, jnp.ones(rows.shape, bf16)], axis=1)


def fill_weights(edge_out, node_out, w_out, w_node_out, spread_of):
    for weights, into in ((edge_out, w_out), (node_out, w_node_out)):
        wide = weights[...].astype(f32)
        centred = (wide - jnp.mean(wide, axis=1, keepdims=True)).astype(bf16)
        into[...] = jnp.zeros_like(into)
        into[:LANES, :LANES] = centred
        into[LANES:, LANES:] = centred
    shape = spread_of.shape
    same = (lax.broadcasted_iota(jnp.int32, shape, 0) < LANES) == (lax.broadcasted_iota(jnp.int32, shape, 1) < LANES)
    spread_of[...] = jnp.where(same, 1.0 / LANES, 0.0).astype(bf16)


weight_scratch = [pltpu.VMEM((2 * LANES, 2 * LANES), bf16)] * 4


weight_specs = ["level"] * 5


def edge_first(picks, receiver_part, edge_rows, sender_part, w_edge):
    before = mm_first(picks, receiver_part) + mm(edge_rows, w_edge)
    return side_by_side(jnp.maximum(before + sender_part, 0.0).astype(bf16))


def edge_sums(picks, message, gain):
    half = picks.shape[1] // 2
    summed = mm(picks[:, :half], message[:, :LANES]) + mm(picks[:, half:], message[:, LANES:])
    return (summed * gain).astype(bf16)


def node_first(node_rows, summed, w_node):
    hidden = mm(jnp.concatenate([node_rows, summed], axis=1), w_node)
    return side_by_side(jnp.maximum(hidden, 0.0).astype(bf16))


def node_last(node_rows, update, gain):
    update = jnp.concatenate([update[:, :LANES], update[:, LANES:]], axis=0)
    return (node_rows.astype(f32) + update * gain).astype(bf16)


def border_kernel(place_ref, index_ref, x_ref, a_ref, b_ref, table, buffer):
    table[...] = x_ref[...].astype(f32)
    count = a_ref.shape[0]
    for side in range(2):
        gather_rows(lambda j: index_ref[0, side, j], table, buffer, count, side * count)
    a_ref[...] = buffer[aligned(count * place_ref[0], count), :].astype(bf16)
    b_ref[...] = buffer[aligned(count * (1 - place_ref[0]), count), :].astype(bf16)


def fill_border(x_ref, place_ref, from_a, from_b, edge_in, table, w_pairs):
    w_s = edge_in[:LANES, :]
    w_pairs[...] = jnp.zeros_like(w_pairs)
    w_pairs[:LANES, :LANES] = w_s
    w_pairs[LANES:, LANES:] = w_s
    count, border = x_ref.shape[0], from_a.shape[0]
    half = border // 2
    for rows, first, scale in (
        (from_a, count + place_ref[0] * border, None),
        (from_b, count + (1 - place_ref[0]) * border, place_ref[1].astype(f32)),
    ):
        both = mm(side_by_side(rows[...]), w_pairs[...])
        if scale is not None:
            both = both * scale
        table[aligned(first, half), :] = both[:, :LANES]
        table[aligned(first + half, half), :] = both[:, LANES:]


def fill_own(x_ref, edge_in, table, receiver_part):
    both = mm(x_ref[...], jnp.concatenate([edge_in[:LANES, :], edge_in[LANES : 2 * LANES, :]], axis=1))
    table[: x_ref.shape[0], :] = both[:, :LANES]
    receiver_part[...] = both[:, LANES:].astype(bf16)


def prepare_kernel(x_ref, edge_in, edge_out, node_in, node_out, gain_ref, sender_part, receiver_part):
    fill_own(x_ref, edge_in, sender_part, receiver_part)


def fine_kernel(
    place_ref, pool_index, sender_ref, edge_ref, x_ref, from_a, from_b, sender_part,
    receiver_part, receiver_ref, edge_in, edge_out, node_in, node_out, gain_ref,
    new_ref, a_ref, b_ref,
    table, new32, buffer, aggregate, node_hidden,
    gathered0, gathered1, hidden0, hidden1, message0, message1,
    index0, index1, index2, index3, index_sem, w_out, w_node_out, spread_of, w_pairs,
):
    gathered, hidden, message = (gathered0, gathered1), (hidden0, hidden1), (message0, message1)
    indices = (index0, index1, index2, index3)
    block = gathered0.shape[0]
    blocks = receiver_ref.shape[0]
    groups = blocks // GROUP
    nodes = x_ref.shape[0] // blocks
    group_nodes = GROUP * nodes
    gain, node_gain = gain_ref[0:1, :], gain_ref[1:2, :]

    def index_copy(t, k):
        at = aligned(jnp.minimum(t, blocks - 1) * block, block)
        return pltpu.make_async_copy(sender_ref.at[at], indices[k], index_sem.at[k])

    def gather_block(k, into):
        gather_rows(lambda j: indices[k][j], table, into, block)

    for k in range(GROUP):
        index_copy(k, k).start()
    fill_weights(edge_out, node_out, w_out, w_node_out, spread_of)
    table[: x_ref.shape[0], :] = sender_part[...]
    fill_border(x_ref, place_ref, from_a, from_b, edge_in, table, w_pairs)
    index_copy(0, 0).wait()
    gather_block(0, gathered0)

    def picks_of(t):
        t = jnp.maximum(t, 0)
        slot = lax.broadcasted_iota(jnp.int32, (1, block), 1) + t * block
        return match_rows(jnp.where(slot < place_ref[2], receiver_ref[t] - t * nodes, -1), nodes)

    def group_step(g, last):
        for k in range(GROUP):
            t = g * GROUP + k
            here, before = k % 2, (k + 1) % 2
            if not last:
                later = (k + 1) % GROUP
                index_copy(t + 1, later).wait()
                index_copy(t + GROUP, k).start()
            keep = {}
            done = jnp.maximum(g - 1, 0)
            rows = aligned(done * group_nodes, group_nodes)

            def pick():
                if not last:
                    keep["picks"] = picks_of(t)
                if not last or k < 2:
                    keep["earlier"] = picks_of(t - 2)

            def multiply_first():
                if not last:
                    keep["before"] = mm_first(
                        keep["picks"], receiver_part[aligned(t * nodes, nodes), :]
                    ) + mm(edge_ref[aligned(t * block, block), :], edge_in[2 * LANES :, :])
                if not last or k < 1:
                    keep["centred"] = mm(hidden[before][...], w_out[...])
                if k == 2:
                    node_hidden[...] = node_first(x_ref[rows, :], aggregate[...], node_in[...])
                if k == 3:
                    keep["node_centred"] = mm(node_hidden[...], w_node_out[...])

            def rectify():
                if not last:
                    rows = jnp.maximum(keep["before"] + gathered[here][...], 0.0)
                    hidden[here][...] = side_by_side(rows.astype(bf16))
                if not last or k < 1:
                    keep["squares"] = (keep["centred"] * keep["centred"]).astype(bf16)
                if k == 3:
                    keep["node_squares"] = (keep["node_centred"] * keep["node_centred"]).astype(bf16)

            def multiply_last():
                if not last or k < 1:
                    keep["spread"] = mm(keep["squares"], spread_of[...])
                if not last or k < 2:
                    into = (k - 2) % GROUP * nodes
                    aggregate[into : into + nodes, :] = edge_sums(keep["earlier"], message[here][...], gain)
                if k == 3:
                    keep["node_spread"] = mm(keep["node_squares"], spread_of[...])

            def scale():
                if not last or k < 1:
                    message[before][...] = (keep["centred"] * lax.rsqrt(keep["spread"] + epsilon)).astype(bf16)
                if k == 3:
                    update = keep["node_centred"] * lax.rsqrt(keep["node_spread"] + epsilon)
                    new_rows = node_last(x_ref[rows, :], update, node_gain)
                    new_ref[rows, :] = new_rows
                    new32[rows, :] = new_rows.astype(f32)

            cuts = (0, *SPLIT, block)
            for i, step in enumerate((pick, multiply_first, rectify, multiply_last, scale)):
                step()
                if not last:
                    gather_rows(
                        lambda j: indices[later][cuts[i] + j], table, gathered[before],
                        cuts[i + 1] - cuts[i], cuts[i],
                    )
    def loop_step(g, carry):
        group_step(g, False)
        return carry

    lax.fori_loop(0, groups, loop_step, 0)
    group_step(groups, True)
    for k in range(1, GROUP):
        index_copy(blocks + k, k).wait()
    count = a_ref.shape[0]
    for side in range(2):
        gather_rows(lambda j: pool_index[0, side, j], new32, buffer, count, side * count)
    a_ref[...] = buffer[aligned(count * place_ref[0], count), :].astype(bf16)
    b_ref[...] = buffer[aligned(count * (1 - place_ref[0]), count), :].astype(bf16)


def local_pool_kernel(new_ref, parent_ref, weight_ref, sums_ref):
    groups, _, size = parent_ref.shape
    total = 0.0
    for g in range(groups):
        shares = match_rows(parent_ref[g], sums_ref.shape[0], weight_ref[g])
        total += mm(shares, with_ones(new_ref[g * size : (g + 1) * size, :]))
    sums_ref[...] = total


def pool_kernel(
    place_ref, border_index, sums_ref, from_a, from_b, target_ref, weight_ref,
    coarse_ref, a_ref, b_ref, table, buffer,
):
    count = sums_ref.shape[0]
    total = sums_ref[...]
    for side, rows in ((place_ref[0], from_a), (1 - place_ref[0], from_b)):
        shares = match_rows(target_ref[side], count, weight_ref[side])
        total += mm(shares, with_ones(rows[...]))
    coarse = (total[:, :LANES] / total[:, LANES:]).astype(bf16)
    coarse_ref[...] = coarse
    table[...] = coarse.astype(f32)
    border = a_ref.shape[0]
    for side in range(2):
        gather_rows(lambda j: border_index[0, side, j], table, buffer, border, side * border)
    a_ref[...] = buffer[aligned(border * place_ref[0], border), :].astype(bf16)
    b_ref[...] = buffer[aligned(border * (1 - place_ref[0]), border), :].astype(bf16)


def coarse_kernel(
    place_ref, sender_ref, edge_ref, x_ref, from_a, from_b, receiver_ref, parent_ref, weight_ref,
    edge_in, edge_out, node_in, node_out, gain_ref,
    new_ref, own_ref, a_ref, b_ref,
    table, receiver_part, gathered, aggregate, shares_sum, w_out, w_node_out, spread_of, w_pairs,
):
    blocks, _, block = receiver_ref.shape
    nodes = x_ref.shape[0] // blocks
    fill_weights(edge_out, node_out, w_out, w_node_out, spread_of)
    fill_own(x_ref, edge_in, table, receiver_part)
    fill_border(x_ref, place_ref, from_a, from_b, edge_in, table, w_pairs)
    keep = {}

    def gather_part(t, part):
        if t < blocks:
            begin = t * block + part * block // 4
            gather_rows(lambda j: sender_ref[begin + j], table, gathered, block // 4, begin)

    def first(t):
        own, at = slice(t * nodes, (t + 1) * nodes), slice(t * block, (t + 1) * block)
        keep["picks", t] = match_rows(receiver_ref[t] - t * nodes, nodes)
        keep["pairs", t] = edge_first(
            keep["picks", t], receiver_part[own, :], edge_ref[at, :], gathered[at, :], edge_in[2 * LANES :, :]
        )

    def second(t):
        keep["centred", t] = mm(keep["pairs", t], w_out[...])

    def third(t):
        centred = keep["centred", t]
        spread = mm((centred * centred).astype(bf16), spread_of[...])
        keep["message", t] = (centred * lax.rsqrt(spread + epsilon)).astype(bf16)

    def sum_edges(t):
        own = slice(t * nodes, (t + 1) * nodes)
        aggregate[own, :] = edge_sums(keep["picks", t], keep["message", t], gain_ref[0:1, :])

    for part in range(4):
        gather_part(0, part)
    for tick in range(blocks + 3):
        for part, (stage, lag) in enumerate(((first, 0), (second, 1), (third, 2), (sum_edges, 3))):
            if 0 <= tick - lag < blocks:
                stage(tick - lag)
            gather_part(tick + 1, part)
    pairs = node_first(x_ref[...], aggregate[...], node_in[...])
    new_rows = node_last(x_ref[...], normed_pairs(pairs, w_node_out[...], spread_of[...]), gain_ref[1:2, :])
    new_ref[...] = new_rows
    share = x_ref.shape[0] // 8
    size = own_ref.shape[0]
    shares = match_rows(parent_ref[...] - (place_ref[3] - 1) * share, 3 * share, weight_ref[...])
    sums = mm(shares, new_rows)
    rest = jnp.zeros((LANES - share, shares.shape[1]), bf16)
    for i in range(3):
        at = slice(i * share, (i + 1) * share)
        shares_sum[i * size : i * size + share, :] = sums[at]
        shares_sum[i * size + share : (i + 1) * size, :] = lax.dot_general(
            jnp.ones((size - share, shares.shape[1]), bf16), jnp.concatenate([shares[at], rest], axis=0),
            (((1,), (1,)), ((), ())), preferred_element_type=f32,
        )
    own_ref[...] = shares_sum[size : 2 * size, :]
    a_ref[...] = shares_sum[aligned(2 * size * place_ref[0], size), :]
    b_ref[...] = shares_sum[aligned(2 * size * (1 - place_ref[0]), size), :]


def lift_kernel(parent_ref, picks_ref):
    groups, _, size = parent_ref.shape
    for g in range(groups):
        picks_ref[g * size : (g + 1) * size, :] = match_rows(parent_ref[g], picks_ref.shape[1]).T


def top_kernel(
    place_ref, sender_ref, picks_ref, edge_ref, gathered_in, receiver_ref, parent_ref, coarse_ref,
    fine_ref, edge_in, edge_out, node_in, node_out, gain_ref,
    fine_out, coarse_out,
    table, top_rows, gathered, w_out, w_node_out, spread_of, w_pairs,
):
    chunk = coarse_ref.shape[0]
    chunks = fine_ref.shape[0] // chunk
    tile = receiver_ref.shape[2]
    share = tile // 2
    nodes = 3 * share
    block = 3 * tile
    parts = gathered_in.shape[0] // share
    me, first = place_ref[3], place_ref[4]
    fill_weights(edge_out, node_out, w_out, w_node_out, spread_of)
    sender_part = mm(gathered_in[...], edge_in[:LANES, :])
    for q in range(parts):
        at = aligned((q ^ me) * share, share)
        table[at, :] = sender_part[q * share : (q + 1) * share, :]
        top_rows[at, :] = gathered_in[q * share : (q + 1) * share, :]
    window = top_rows[pl.ds(pl.multiple_of(first * share, share), nodes), :]
    gather_rows(lambda j: sender_ref[first * tile + j], table, gathered, block)
    ids = jnp.concatenate([receiver_ref[first + i] for i in range(3)], axis=1) - first * share
    matches = match_rows(ids, nodes)
    pairs = edge_first(
        matches, mm(window, edge_in[LANES : 2 * LANES, :]).astype(bf16),
        edge_ref[pl.ds(pl.multiple_of(first * tile, tile), block), :], gathered[...], edge_in[2 * LANES :, :],
    )
    message = normed_pairs(pairs, w_out[...], spread_of[...]).astype(bf16)
    pairs = node_first(window, edge_sums(matches, message, gain_ref[0:1, :]), node_in[...])
    top_new = node_last(window, normed_pairs(pairs, w_node_out[...], spread_of[...]), gain_ref[1:2, :])
    up = mm_first(match_rows(parent_ref[...] - first * share, nodes), top_new)
    coarse = (coarse_ref[...].astype(f32) + up).astype(bf16)
    coarse_out[...] = coarse
    for i in range(chunks):
        at = slice(i * chunk, (i + 1) * chunk)
        fine_out[at, :] = (fine_ref[at, :].astype(f32) + mm(picks_ref[at, :], coarse)).astype(bf16)


def call(kernel, name, outs, kinds, scratch, operands, level=None, us=1.0):
    def with_level(*refs):
        kernel(*[
            ref.at[level] if i < len(kinds) and kinds[i] == "level" else ref for i, ref in enumerate(refs)
        ])

    spaces = {whole_smem: pltpu.SMEM, left_in_hbm: pl.ANY}
    return pl.pallas_call(
        with_level,
        name=name,
        out_shape=outs,
        in_specs=[pl.BlockSpec(memory_space=spaces.get(kind, pltpu.VMEM)) for kind in kinds],
        out_specs=jax.tree.map(lambda _: pl.BlockSpec(memory_space=pltpu.VMEM), outs),
        scratch_shapes=scratch,
        cost_estimate=pl.CostEstimate(flops=int(us * 10**9), bytes_accessed=0, transcendentals=0),
        compiler_params=pltpu.CompilerParams(vmem_limit_bytes=VMEM_LIMIT),
    )(*operands)


def rows_of(count, dtype=bf16, width=LANES):
    return jax.ShapeDtypeStruct((count, width), dtype)


def swap_with_neighbours(for_a, for_b):
    count = lax.axis_size("dom")
    pairs_a = [(i, i ^ 1) for i in range(count)]
    pairs_b = [(i, (i + 1) % count) for i in range(1, count, 2)]
    pairs_b += [(j, i) for i, j in pairs_b]
    return lax.ppermute(for_a, "dom", pairs_a), lax.ppermute(for_b, "dom", pairs_b)


def gather_all(rows):
    count = lax.axis_size("dom")
    steps = []
    stride = 1
    while stride < count:
        radix = 4 if stride * 4 <= count else 2
        steps.append((stride, radix))
        stride *= radix
    blocks = rows[None]
    for stride, radix in reversed(steps):
        taken = [blocks] + [
            lax.ppermute(blocks, "dom", [(i, i ^ (j * stride)) for i in range(count)])
            for j in range(1, radix)
        ]
        blocks = jnp.stack(taken, axis=1).reshape((-1,) + rows.shape)
    return blocks


def body(
    fine_latent, fine_edges, fine_sender, fine_receiver, edge_count, fine_border, pool_rows, pool_target,
    pool_weight, fine_parent, fine_weight, coarse_edges, coarse_sender, coarse_receiver, coarse_border,
    coarse_parent, coarse_weight, top_edges, top_sender, top_receiver, edge_in, edge_out, node_in, node_out,
    norm_gain,
):
    count = lax.axis_size("dom")
    me = lax.axis_index("dom").astype(jnp.int32)
    inner = jnp.where((me == 0) | (me == count - 1), 0, 1).astype(jnp.int32)
    place = jnp.stack([1 - me % 2, inner, edge_count[0], me, jnp.clip(me - 1, 0, count - 3)])
    weights = (edge_in, edge_out, node_in, node_out, norm_gain)

    fine_total = fine_latent.shape[0]
    edge_total = fine_sender.shape[0]
    coarse_total = coarse_parent.shape[0]
    border = fine_border.shape[2]
    slots = pool_rows.shape[2]
    nodes = LANES
    block = nodes * edge_total // fine_total
    blocks = edge_total // block
    groups = blocks // GROUP

    with jax.named_scope("fine_border_rows"):
        for_a, for_b = call(
            border_kernel, "border_rows", [rows_of(border), rows_of(border)],
            [whole_smem, whole_smem, whole_vmem],
            [pltpu.VMEM((fine_total, LANES), f32), pltpu.VMEM((2 * border, LANES), f32)],
            (place, fine_border, fine_latent),
            us=3.0,
        )
        from_a, from_b = swap_with_neighbours(for_a, for_b)
        prepared = call(
            prepare_kernel, "fine_prepare", [rows_of(fine_total, f32), rows_of(fine_total)],
            [whole_vmem] + weight_specs, [], (fine_latent,) + weights, level=0, us=2.0,
        )
        lift_picks = call(
            lift_kernel, "lift_picks", rows_of(fine_total, bf16, coarse_total), [whole_vmem], [],
            (fine_parent.reshape(fine_total // coarse_total, 1, coarse_total),),
            us=3.0,
        )

    with jax.named_scope("fine_step"):
        fine_new, for_a, for_b = call(
            fine_kernel, "fine_step",
            [rows_of(fine_total), rows_of(slots), rows_of(slots)],
            [whole_smem, whole_smem, left_in_hbm] + [whole_vmem] * 7 + weight_specs,
            [
                pltpu.VMEM((fine_total + 2 * border, LANES), f32),
                pltpu.VMEM((fine_total, LANES), f32),
                pltpu.VMEM((2 * slots, LANES), f32),
                pltpu.VMEM((GROUP * nodes, LANES), bf16),
                pltpu.VMEM((GROUP * nodes // 2, 2 * LANES), bf16),
            ]
            + [pltpu.VMEM((block, LANES), f32)] * 2
            + [pltpu.VMEM((block // 2, 2 * LANES), bf16)] * 4
            + [pltpu.SMEM((block,), jnp.int32)] * GROUP
            + [pltpu.SemaphoreType.DMA((GROUP,))]
            + weight_scratch,
            (
                place, pool_rows, fine_sender, fine_edges, fine_latent, from_a, from_b, *prepared,
                fine_receiver.reshape(blocks, 1, block),
            )
            + weights,
            level=0,
            us=24.0,
        )
        from_a, from_b = swap_with_neighbours(for_a, for_b)
        by_group = (groups, 1, GROUP * nodes)
        local_sums = call(
            local_pool_kernel, "local_pool_step", rows_of(coarse_total, f32, 2 * LANES), [whole_vmem] * 3, [],
            (fine_new, fine_parent.reshape(by_group), fine_weight.reshape(by_group)),
            us=2.0,
        )

    with jax.named_scope("coarse_input"):
        border1 = coarse_border.shape[2]
        coarse_in, for_a, for_b = call(
            pool_kernel, "coarse_input",
            [rows_of(coarse_total), rows_of(border1), rows_of(border1)],
            [whole_smem, whole_smem] + [whole_vmem] * 5,
            [pltpu.VMEM((coarse_total, LANES), f32), pltpu.VMEM((2 * border1, LANES), f32)],
            (
                place, coarse_border, local_sums, from_a, from_b,
                pool_target.reshape(2, 1, slots), pool_weight.reshape(2, 1, slots),
            ),
        )
        from_a, from_b = swap_with_neighbours(for_a, for_b)

    with jax.named_scope("coarse_step"):
        edge_total1 = coarse_sender.shape[0]
        block1 = LANES * edge_total1 // coarse_total
        blocks1 = edge_total1 // block1
        share = coarse_total // 8
        coarse_new, own, for_a, for_b = call(
            coarse_kernel, "coarse_step",
            [rows_of(coarse_total)] + [rows_of(share + 8, f32)] * 3,
            [whole_smem, whole_smem] + [whole_vmem] * 7 + weight_specs,
            [
                pltpu.VMEM((coarse_total + 2 * border1, LANES), f32),
                pltpu.VMEM((coarse_total, LANES), bf16),
                pltpu.VMEM((edge_total1, LANES), f32),
                pltpu.VMEM((coarse_total, LANES), bf16),
                pltpu.VMEM((3 * (share + 8), LANES), f32),
            ]
            + weight_scratch,
            (
                place, coarse_sender, coarse_edges, coarse_in, from_a, from_b,
                coarse_receiver.reshape(blocks1, 1, block1), coarse_parent[None, :], coarse_weight[None, :],
            )
            + weights,
            level=1,
            us=4.0,
        )
        from_a, from_b = swap_with_neighbours(for_a, for_b)
        shares = own + from_a + from_b
        top_in = (shares[:share] / shares[share, :share][:, None]).astype(bf16)

    with jax.named_scope("top_step"):
        everyone = gather_all(top_in).reshape(count * share, LANES)
        tile = 2 * share
        window = 3 * tile
        fine_out, coarse_out = call(
            top_kernel, "top_step",
            [rows_of(fine_total), rows_of(coarse_total)],
            [whole_smem, whole_smem] + [whole_vmem] * 7 + weight_specs,
            [
                pltpu.VMEM((count * share, LANES), f32),
                pltpu.VMEM((count * share, LANES), bf16),
                pltpu.VMEM((window, LANES), f32),
            ]
            + weight_scratch,
            (
                place, top_sender, lift_picks, top_edges, everyone,
                top_receiver.reshape(top_receiver.shape[0] // tile, 1, tile), coarse_parent[None, :], coarse_new,
                fine_new,
            )
            + weights,
            level=2,
            us=5.0,
        )
    return (fine_out, coarse_out)


def solution(mesh):
    row = ("groups", "dom")
    return jax.shard_map(
        body,
        mesh=mesh,
        in_specs=(
            P(row, None), P(row, None), P(row), P(row), P(row), P(row, None, None), P(row, None, None),
            P(row, None, None), P(row, None, None), P(row), P(row), P(row, None), P(row), P(row),
            P(row, None, None), P(row), P(row), P("groups", None), P("groups"), P("groups"), P(), P(), P(), P(),
            P(),
        ),
        out_specs=(P(row, None), P(row, None)),
        check_vma=False,
    )
```
